512 devices in a mesh: seq: 128 (over z, y, core), head: 4 (over x).
Axes of the slice: x: 4, y: 8, z: 8, core: 2. Of those that a mesh axis runs over, the one named last changes fastest.
Arguments:
- queries: bfloat16 [16384, 32, 128], P('seq', 'head')
- keys: bfloat16 [16384, 8, 128], P('seq', 'head')
- values: bfloat16 [16384, 8, 128], P('seq', 'head'), may hold values from -6 to 6
- mem_keys: bfloat16 [131072, 8, 128], P('seq', 'head')
- mem_values: bfloat16 [131072, 8, 128], P('seq', 'head'), may hold values from -6 to 6
- mem_ids: int32 [8, 128, 32], P('head', 'seq'), may hold values from 0 to 2047, as said below
- gate_logits: float32 [32], P('head'), may hold values from -3 to 3
Outputs:
- attended: bfloat16 [16384, 4096], P(('seq', 'head'))
The draws below stay inside these ranges and needn't reach their ends.
Inputs may be any that keep to these rules, and one draw needn't show every extreme that they name: `mem_ids`: ids of memory blocks. The 32 ids of one list differ. Over the 1 lists of the query blocks of one index of seq and one kv head, at most 1 distinct ids lie in any one aligned range of 16 blocks, and some range holds exactly 1.
All inputs are finite; a program needn't handle non-finite values.
Results may differ from the reference program's by a relative error of at most 0.011.
Values may be sent and summed in bfloat16 or wider, within the bound.
No kernel may reach another device: no remote copies, remote signals or barrier semaphores. Data moves between devices by JAX's collectives and lax.ppermute only.
A program may use at most 64 MiB of HBM per device.

```python
import jax
import jax.numpy as jnp
from jax import lax

HEADS = 32
KV_HEADS = 8
HEAD_DIM = 128
TOK_DEV = 128
QBLK = 128
BLOCK = 64
TOPK = 32
TOKENS = 16384
WINDOW = 128
MEMORY = 131072
BLK_DEV = 16
BLOCKS = 2048
QBD = 1
QBLOCKS = 128
CAP = 1


def drawn_keys(key, rows, heads):
    base = jnp.clip(jax.random.normal(key, (rows, heads, HEAD_DIM), jnp.float32), -4.0, 4.0)
    return base


def draw_queries(key, part):
    key = jax.random.fold_in(key, 1)
    base = jnp.clip(jax.random.normal(key, (TOKENS, HEADS, HEAD_DIM), jnp.float32), -4.0, 4.0)
    result = base
    return result.astype(jnp.bfloat16)


def draw_keys(key, part):
    key = jax.random.fold_in(key, 2)
    return drawn_keys(key, TOKENS, KV_HEADS).astype(jnp.bfloat16)


def draw_mem_keys(key, part):
    key = jax.random.fold_in(key, 3)
    return drawn_keys(key, MEMORY, KV_HEADS).astype(jnp.bfloat16)


def draw_mem_ids(key, part):
    key = jax.random.fold_in(key, 4)
    owners = QBLOCKS // QBD
    slots = owners * CAP
    hotness = jax.random.randint(jax.random.fold_in(key, 50), (owners,), 0, 4)
    slot_owner = jnp.arange(slots) // CAP

    def draw_list(head_index, device):
        subkey = jax.random.fold_in(jax.random.fold_in(key, head_index), device + 100)
        local_ids = jnp.arange(BLK_DEV)[None, :]
        owner_ids = jnp.arange(owners)[:, None]
        ordering = jax.random.randint(jax.random.fold_in(subkey, 1), (owners, BLK_DEV), 0, 2 ** 20) * BLK_DEV + local_ids
        forced = (device == 0) & ((owner_ids == owners - 1) & (local_ids == BLK_DEV - 1) | (owner_ids == 0) & (local_ids == 0))
        ordering = jnp.where(forced, -1, ordering)
        chosen = jnp.argsort(ordering, axis=1, stable=True)[:, :CAP]
        candidates = (owner_ids * BLK_DEV + chosen).reshape(slots)
        ranking = jax.random.randint(jax.random.fold_in(subkey, 2), (QBD, slots), 0, 2 ** 16) + hotness[slot_owner][None, :] * 2 ** 14
        favoured = (device == 0) & ((jnp.arange(slots) == 0) | (jnp.arange(slots) == (owners - 1) * CAP))
        ranking = ranking + jnp.where(favoured, 2 ** 18, 0)[None, :]
        ranking = ranking * slots + jnp.arange(slots)[None, :]
        picked = lax.top_k(ranking, TOPK)[1]
        return candidates[picked]
    per_device = jax.vmap(draw_list, in_axes=(None, 0))
    every = jax.vmap(per_device, in_axes=(0, None))(jnp.arange(KV_HEADS), jnp.arange(owners))
    return every.reshape(KV_HEADS, QBLOCKS, TOPK).astype(jnp.int32)


def block_levels(rng, shape, cuts, least, top_value):
    loudness, own = 1.0, jax.random.fold_in(rng, 6)
    for position, blocks in cuts:
        steps = jnp.exp(jax.random.uniform(jax.random.fold_in(own, position), (blocks,), jnp.float32, least / len(cuts), top_value / len(cuts)))
        loudness = loudness * jnp.repeat(steps, shape[position] // blocks).reshape([-1 if axis == position else 1 for axis in range(len(shape))])
    return loudness


def gaussian(rng, dims, spread, most, pieces=(), kind=jnp.bfloat16):
    values = jax.random.normal(rng, dims, jnp.float32) * spread
    if len(pieces) > 0:
        values = block_levels(rng, dims, pieces, -0.22, 0.18) * values
    return jnp.clip(values, min=-most, max=most).astype(kind)


def setup_inputs(seed: int = 0) -> dict:
    arg_keys = jax.random.split(jax.random.key(seed), 8)
    queries = draw_queries(jax.random.fold_in(arg_keys[7], 71), 0)
    keys = draw_keys(jax.random.fold_in(arg_keys[7], 71), 0)
    values = gaussian(arg_keys[2], (TOKENS, KV_HEADS, HEAD_DIM), 1.0, 6.0, ((0, 128), (1, 4)))
    mem_keys = draw_mem_keys(jax.random.fold_in(arg_keys[7], 71), 0)
    mem_values = gaussian(arg_keys[4], (MEMORY, KV_HEADS, HEAD_DIM), 1.0, 6.0, ((0, 128), (1, 4)))
    mem_ids = draw_mem_ids(jax.random.fold_in(arg_keys[7], 71), 0)
    gate_logits = jnp.clip(jax.random.uniform(arg_keys[6], (HEADS,), jnp.float32, -3.0, 3.0) * block_levels(arg_keys[6], (HEADS,), ((0, 4),), -0.4, 0.0), -3.0, 3.0)
    return dict(queries=queries, keys=keys, values=values, mem_keys=mem_keys, mem_values=mem_values, mem_ids=mem_ids, gate_logits=gate_logits)


def attend(query_rows, key_rows, value_rows, allowed):
    score_scale = HEAD_DIM ** -0.5
    scores = jnp.einsum('qkgd,ksd->kgqs', query_rows.astype(jnp.float32), key_rows.astype(jnp.float32)) * score_scale
    if allowed is not None:
        scores = jnp.where(allowed[None, None, :, :], scores, -1e30)
    highest = jnp.max(scores, axis=3, keepdims=True)
    expo = jnp.exp(scores - highest)
    weights = (expo / jnp.sum(expo, axis=3, keepdims=True)).astype(jnp.bfloat16)
    return jnp.einsum('kgqs,ksd->qkgd', weights.astype(jnp.float32), value_rows.astype(jnp.float32))


def reference(queries, keys, values, mem_keys, mem_values, mem_ids, gate_logits):
    group = HEADS // KV_HEADS
    zero_rows = jnp.zeros((TOK_DEV, KV_HEADS, HEAD_DIM), keys.dtype)
    pad_keys = jnp.concatenate([zero_rows, keys], axis=0)
    pad_values = jnp.concatenate([zero_rows, values], axis=0)
    cache_keys = mem_keys.reshape(BLOCKS, BLOCK, KV_HEADS, HEAD_DIM).transpose(2, 0, 1, 3)
    cache_values = mem_values.reshape(BLOCKS, BLOCK, KV_HEADS, HEAD_DIM).transpose(2, 0, 1, 3)
    head_rows = jnp.arange(KV_HEADS, dtype=jnp.int32)[:, None]
    gate = jax.nn.sigmoid(gate_logits.astype(jnp.float32)).reshape(KV_HEADS, group)[None, :, :, None]
    span = TOK_DEV + QBLK

    def one_block(block_index):
        start = block_index * QBLK
        query_rows = lax.dynamic_slice_in_dim(queries, start, QBLK, 0).reshape(QBLK, KV_HEADS, group, HEAD_DIM)
        near_keys = lax.dynamic_slice_in_dim(pad_keys, start, span, 0).transpose(1, 0, 2)
        near_values = lax.dynamic_slice_in_dim(pad_values, start, span, 0).transpose(1, 0, 2)
        key_pos = start - TOK_DEV + jnp.arange(span, dtype=jnp.int32)
        query_pos = start + jnp.arange(QBLK, dtype=jnp.int32)
        allowed = (key_pos[None, :] <= query_pos[:, None]) & (key_pos[None, :] > query_pos[:, None] - WINDOW) & (key_pos[None, :] >= 0)
        window = attend(query_rows, near_keys, near_values, allowed)
        chosen = lax.dynamic_index_in_dim(mem_ids, block_index, 1, keepdims=False)
        far_keys = cache_keys[head_rows, chosen].reshape(KV_HEADS, TOPK * BLOCK, HEAD_DIM)
        far_values = cache_values[head_rows, chosen].reshape(KV_HEADS, TOPK * BLOCK, HEAD_DIM)
        memory = attend(query_rows, far_keys, far_values, None)
        mixed = gate * memory + (1.0 - gate) * window
        return mixed.reshape(QBLK, HEADS * HEAD_DIM).astype(jnp.bfloat16)

    blocks_out = lax.map(one_block, jnp.arange(QBLOCKS, dtype=jnp.int32))
    return blocks_out.reshape(TOKENS, HEADS * HEAD_DIM)
```

```python
import functools
import math

import jax
import jax.numpy as jnp
from jax import lax
from jax.experimental import pallas as pl
from jax.experimental.pallas import tpu as pltpu
from jax.sharding import Mesh
from jax.sharding import PartitionSpec as P

Z, Y, X = 8, 8, 4
LINE = 8
BLOCK = 64
TOPK = 32
BLK_DEV = 16
HEAD = 128
ROWS = 512
QROWS = ROWS + 16
CHUNK = 2 * BLK_DEV * BLOCK
CHUNKS = 2 * LINE
LISTS = 2 * LINE
OROWS = HEAD + 16
STEP = 4
LOWEST = -3.0e38
EXPO = HEAD**-0.5 * math.log2(math.e)
SEQ = ("z", "y", "core")


def seq_index(z, y, core):
    return (z * Y + y) * 2 + core


Y_LINES = [[[seq_index(z, y, core) for y in range(Y)] for z in range(Z)] for core in range(2)]
Z_LINES = [[[seq_index(z, y, core) for z in range(Z)] for y in range(Y)] for core in range(2)]
KV_LINES = Y_LINES[0] + Z_LINES[1]
Q_LINES = Z_LINES[0] + Y_LINES[1]


def along(value, by):
    pairs = [(line[i], line[(i + by) % LINE]) for line in KV_LINES for i in range(LINE)]
    return lax.ppermute(value, SEQ, pairs)


def window_kernel(first_ref, q_ref, k_ref, v_ref, o_ref):
    for rc in range(2):
        s = lax.dot_general(
            k_ref[pl.ds(128 * rc, 256), :],
            q_ref[rc, :ROWS, :],
            (((1,), (1,)), ((), ())),
            preferred_element_type=jnp.float32,
        )
        kpos = lax.broadcasted_iota(jnp.int32, s.shape, 0) - 128
        qpos = lax.broadcasted_iota(jnp.int32, s.shape, 1) & 127
        allowed = (kpos <= qpos) & (kpos > qpos - 128)
        if rc == 0:
            allowed = allowed & ((kpos >= 0) | (first_ref[0] == 0))
        s = jnp.where(allowed, s, LOWEST)
        top = jnp.max(s, axis=0, keepdims=True)
        p = jnp.exp2((s - top) * EXPO)
        total = jnp.sum(p, axis=0, keepdims=True)
        out = lax.dot_general(
            v_ref[pl.ds(128 * rc, 256), :],
            p.astype(jnp.bfloat16),
            (((0,), (0,)), ((), ())),
            preferred_element_type=jnp.float32,
        )
        o_ref[rc] = out / total


def memory_kernel(count_ref, place_ref, q_ref, *rest):
    chunks = rest[:CHUNKS]
    o_ref, kv, acc, top_s, sum_s, sems = rest[CHUNKS:]
    copies = [
        pltpu.make_async_copy(chunks[j], kv.at[pl.ds(j * CHUNK, CHUNK)], sems.at[j])
        for j in range(CHUNKS)
    ]
    for copy in copies:
        copy.start()
    for copy in copies:
        copy.wait()

    def one_list(index, carry):
        count = count_ref[index]
        top_s[...] = jnp.full((1, ROWS), LOWEST, jnp.float32)
        sum_s[...] = jnp.zeros((1, ROWS), jnp.float32)
        acc[...] = jnp.zeros((HEAD, ROWS), jnp.float32)

        def one_step(step, inner):
            places = [pl.multiple_of(place_ref[index * BLK_DEV + step * STEP + i], BLOCK) for i in range(STEP)]
            keys = jnp.concatenate([kv[pl.ds(at, BLOCK), :] for at in places], axis=0)
            values = jnp.concatenate(
                [kv[pl.ds(at + BLK_DEV * BLOCK, BLOCK), :] for at in places], axis=0
            )
            s = lax.dot_general(
                keys, q_ref[index, :ROWS, :], (((1,), (1,)), ((), ())), preferred_element_type=jnp.float32
            )
            rows = lax.broadcasted_iota(jnp.int32, s.shape, 0)
            s = jnp.where(rows < (count - step * STEP) * BLOCK, s, LOWEST)
            top = jnp.maximum(top_s[...], jnp.max(s, axis=0, keepdims=True))
            p = jnp.exp2((s - top) * EXPO)
            alpha = jnp.exp2((top_s[...] - top) * EXPO)
            sum_s[...] = sum_s[...] * alpha + jnp.sum(p, axis=0, keepdims=True)
            acc[...] = acc[...] * alpha + lax.dot_general(
                values, p.astype(jnp.bfloat16), (((0,), (0,)), ((), ())), preferred_element_type=jnp.float32
            )
            top_s[...] = top
            return inner

        lax.fori_loop(0, (count + STEP - 1) // STEP, one_step, 0)
        total = sum_s[...]
        some = total > 0.0
        safe = jnp.where(some, total, 1.0)
        o_ref[index, :HEAD, :] = (acc[...] / safe).astype(jnp.bfloat16)
        level = jnp.where(some, top_s[...] * EXPO + jnp.log2(safe), LOWEST)
        high = level.astype(jnp.bfloat16).astype(jnp.float32)
        mid = (level - high).astype(jnp.bfloat16).astype(jnp.float32)
        low = level - high - mid
        rows = lax.broadcasted_iota(jnp.int32, (16, ROWS), 0)
        pieces = jnp.where(rows == 0, high, jnp.where(rows == 1, mid, jnp.where(rows == 2, low, 0.0)))
        o_ref[index, HEAD:, :] = pieces.astype(jnp.bfloat16)
        return carry

    lax.fori_loop(0, LISTS, one_list, 0)


def merge_kernel(part_ref, window_ref, gate_ref, o_ref):
    gate = gate_ref[...]
    for rc in range(2):
        levels = []
        for i in range(LINE):
            pieces = part_ref[i, rc, HEAD:, :].astype(jnp.float32)
            levels.append(pieces[0:1, :] + pieces[1:2, :] + pieces[2:3, :])
        top = functools.reduce(jnp.maximum, levels)
        shares = [jnp.exp2(level - top) for level in levels]
        total = functools.reduce(jnp.add, shares)
        mixed = (1.0 - gate) * window_ref[rc]
        scale = gate / total
        for i in range(LINE):
            mixed = mixed + part_ref[i, rc, :HEAD, :].astype(jnp.float32) * (shares[i] * scale)
        for g in range(4):
            flat = mixed[:, g * 128 : (g + 1) * 128].T.astype(jnp.bfloat16)
            for x in range(X):
                o_ref[x * 2 + rc, :, g * 128 : (g + 1) * 128] = flat[x * 32 : (x + 1) * 32, :]


def on_device(queries, keys, values, mem_keys, mem_values, mem_ids, gate_logits):
    z, y, core = lax.axis_index("z"), lax.axis_index("y"), lax.axis_index("core")
    first_core = core == 0

    def mine_and_other(array):
        return jnp.where(first_core, array[0], array[1]), jnp.where(first_core, array[1], array[0])

    def by_core(mine, other):
        return jnp.where(first_core, mine, other), jnp.where(first_core, other, mine)

    mk_mine, mk_other = mine_and_other(mem_keys.transpose(1, 0, 2))
    mv_mine, mv_other = mine_and_other(mem_values.transpose(1, 0, 2))
    chunk_a = jnp.concatenate([mk_mine, mv_mine], axis=0)
    q_mine, q_other = mine_and_other(
        queries.reshape(128, 2, 4, HEAD).transpose(1, 2, 0, 3).reshape(2, ROWS, HEAD)
    )
    ids = jnp.concatenate([mem_ids // 64, mem_ids % 64], axis=2).astype(jnp.bfloat16)
    ids = jnp.pad(ids, ((0, 0), (0, 15), (0, HEAD - 2 * TOPK)))
    ids_mine, ids_other = mine_and_other(ids)
    k_mine, k_other = mine_and_other(keys.transpose(1, 0, 2))
    v_mine, v_other = mine_and_other(values.transpose(1, 0, 2))
    swap = [(0, 1), (1, 0)]
    small = lax.ppermute(
        jnp.concatenate([q_other, ids_other, k_other, v_other], axis=0), "core", swap
    )
    chunk_b = lax.ppermute(jnp.concatenate([mk_other, mv_other], axis=0), "core", swap)

    q_list = jnp.stack(by_core(jnp.concatenate([q_mine, ids_mine], axis=0), small[:QROWS]))
    gathered = lax.all_gather(q_list, SEQ, axis_index_groups=Q_LINES, tiled=True)

    parts = {("a", 0): chunk_a, ("b", 0): chunk_b}
    for hop in range(1, 4):
        for name in ("a", "b"):
            parts[name, -hop % LINE] = along(parts[name, (1 - hop) % LINE], 1)
            parts[name, hop] = along(parts[name, hop - 1], -1)
    parts["a", 4] = along(parts["a", 5], 1)
    parts["b", 4] = along(parts["b", 3], -1)
    chunks = [parts["a", d] for d in range(LINE)] + [parts["b", d] for d in range(LINE)]

    k_first, k_second = by_core(k_mine, small[QROWS : QROWS + 128])
    v_first, v_second = by_core(v_mine, small[QROWS + 128 :])
    chips = Z * Y
    onward = [(2 * i + c, 2 * i + 2 + c) for i in range(chips - 1) for c in range(2)]
    before = lax.ppermute(jnp.concatenate([k_second, v_second], axis=0), SEQ, onward)
    near_keys = jnp.concatenate([before[:128], k_first, k_second], axis=0)
    near_values = jnp.concatenate([before[128:], v_first, v_second], axis=0)
    is_first = ((z == 0) & (y == 0)).astype(jnp.int32).reshape(1)
    window = pl.pallas_call(
        window_kernel,
        out_shape=jax.ShapeDtypeStruct((2, HEAD, ROWS), jnp.float32),
        grid_spec=pltpu.PrefetchScalarGridSpec(
            num_scalar_prefetch=1,
            grid=(1,),
            in_specs=[
                pl.BlockSpec((2, QROWS, HEAD), lambda i, s: (0, 0, 0)),
                pl.BlockSpec((384, HEAD), lambda i, s: (0, 0)),
                pl.BlockSpec((384, HEAD), lambda i, s: (0, 0)),
            ],
            out_specs=pl.BlockSpec((2, HEAD, ROWS), lambda i, s: (0, 0, 0)),
        ),
        compiler_params=pltpu.CompilerParams(vmem_limit_bytes=24 << 20),
        cost_estimate=pl.CostEstimate(
            flops=4 * 2 * ROWS * 256 * HEAD, bytes_accessed=1 << 20, transcendentals=2 * ROWS * 256
        ),
        name="window",
    )(is_first, q_list, near_keys, near_values)

    coded = gathered[:, ROWS, : 2 * TOPK].astype(jnp.int32)
    wanted = coded[:, :TOPK] * 64 + coded[:, TOPK:]
    owner, local = wanted // BLK_DEV, wanted % BLK_DEV
    owner_z, owner_y, owner_core = owner // (2 * Y), (owner // 2) % Y, owner % 2
    here = jnp.where(first_core, owner_z == z, owner_y == y)
    delta = jnp.where(first_core, owner_y - y, owner_z - z) % LINE
    slot = delta + jnp.where(owner_core == core, 0, LINE)
    place = slot * CHUNK + local * BLOCK
    rank = jnp.sum(
        (here[:, None, :] & (jnp.arange(TOPK)[None, None, :] < jnp.arange(TOPK)[None, :, None])).astype(jnp.int32),
        axis=2,
    )
    match = here[:, :, None] & (rank[:, :, None] == jnp.arange(BLK_DEV)[None, None, :])
    places = jnp.sum(jnp.where(match, place[:, :, None], 0), axis=1)
    counts = jnp.sum(here.astype(jnp.int32), axis=1)

    partial = pl.pallas_call(
        memory_kernel,
        out_shape=jax.ShapeDtypeStruct((LISTS, OROWS, ROWS), jnp.bfloat16),
        grid_spec=pltpu.PrefetchScalarGridSpec(
            num_scalar_prefetch=2,
            grid=(1,),
            in_specs=[pl.BlockSpec((LISTS, QROWS, HEAD), lambda i, s, t: (0, 0, 0))]
            + [pl.BlockSpec(memory_space=pl.ANY)] * CHUNKS,
            out_specs=pl.BlockSpec((LISTS, OROWS, ROWS), lambda i, s, t: (0, 0, 0)),
            scratch_shapes=[
                pltpu.VMEM((CHUNKS * CHUNK, HEAD), jnp.bfloat16),
                pltpu.VMEM((HEAD, ROWS), jnp.float32),
                pltpu.VMEM((1, ROWS), jnp.float32),
                pltpu.VMEM((1, ROWS), jnp.float32),
                pltpu.SemaphoreType.DMA((CHUNKS,)),
            ],
        ),
        compiler_params=pltpu.CompilerParams(vmem_limit_bytes=40 << 20),
        cost_estimate=pl.CostEstimate(
            flops=4 * 64 * ROWS * BLOCK * HEAD, bytes_accessed=12 << 20, transcendentals=64 * ROWS * BLOCK
        ),
        name="memory",
    )(counts, places.reshape(-1), gathered, *chunks)

    returned = lax.all_to_all(
        partial, SEQ, split_axis=0, concat_axis=0, axis_index_groups=Q_LINES, tiled=True
    ).reshape(LINE, 2, OROWS, ROWS)
    gate = jax.nn.sigmoid(gate_logits).reshape(2, 4)
    gate = jnp.repeat(jnp.where(first_core, gate[0], gate[1]), 128)[None, :]
    mixed = pl.pallas_call(
        merge_kernel,
        out_shape=jax.ShapeDtypeStruct((2 * X, 32, ROWS), jnp.bfloat16),
        compiler_params=pltpu.CompilerParams(vmem_limit_bytes=24 << 20),
        cost_estimate=pl.CostEstimate(flops=1 << 22, bytes_accessed=4 << 20, transcendentals=1 << 13),
        name="merge",
    )(returned, window, gate)
    rows = lax.all_to_all(mixed, ("head", "core"), split_axis=0, concat_axis=0, tiled=True)
    return rows.transpose(1, 0, 2).reshape(32, 2 * X * ROWS)


def solution(mesh):
    fine = Mesh(mesh.devices.reshape(Z, Y, 2, X), ("z", "y", "core", "head"))
    placed = (
        P(SEQ, "head", None),
        P(SEQ, "head", None),
        P(SEQ, "head", None),
        P(SEQ, "head", None),
        P(SEQ, "head", None),
        P("head", SEQ, None),
        P("head"),
    )
    return jax.shard_map(
        on_device, mesh=fine, in_specs=placed, out_specs=P(SEQ + ("head",), None), check_vma=False
    )
```

```python
import functools
import math

import jax
import jax.numpy as jnp
from jax import lax
from jax.experimental import pallas as pl
from jax.experimental.pallas import tpu as pltpu
from jax.sharding import Mesh
from jax.sharding import PartitionSpec as P

Z, Y, X = 8, 8, 4
LINE = 8
BLOCK = 64
TOPK = 32
BLK_DEV = 16
HEAD = 128
ROWS = 512
QROWS = ROWS + 16
PAIR = 2 * BLOCK
SHARE = BLK_DEV * PAIR
LISTS = 2 * LINE
OROWS = 2 * HEAD + 16
STEP = 4
LOWEST = -3.0e38
EXPO = HEAD**-0.5 * math.log2(math.e)
SEQ = ("z", "y", "core")


def seq_index(z, y, core):
    return (z * Y + y) * 2 + core


Y_LINES = [[[seq_index(z, y, core) for y in range(Y)] for z in range(Z)] for core in range(2)]
Z_LINES = [[[seq_index(z, y, core) for z in range(Z)] for y in range(Y)] for core in range(2)]
KV_LINES = Y_LINES[0] + Z_LINES[1]
Q_LINES = Z_LINES[0] + Y_LINES[1]
Q_PLANES = [[i * X + x for i in line for x in range(X)] for line in Q_LINES]


def shift(value, lines, by):
    return lax.ppermute(value, SEQ, [(line[i], line[(i + by) % LINE]) for line in lines for i in range(LINE)])


def window_kernel(first_ref, gate_ref, q_ref, k_ref, v_ref, o_ref):
    for rc in range(2):
        s = lax.dot_general(
            k_ref[pl.ds(128 * rc, 256), :],
            q_ref[rc * QROWS : rc * QROWS + ROWS, :],
            (((1,), (1,)), ((), ())),
            preferred_element_type=jnp.float32,
        )
        kpos = lax.broadcasted_iota(jnp.int32, s.shape, 0) - 128
        column = lax.broadcasted_iota(jnp.int32, s.shape, 1)
        qpos = (column >> 7) * 32 + (column & 31)
        allowed = (kpos <= qpos) & (kpos > qpos - 128)
        if rc == 0:
            allowed = allowed & ((kpos >= 0) | (first_ref[0] == 0))
        s = jnp.where(allowed, s, LOWEST)
        top = jnp.max(s, axis=0, keepdims=True)
        p = jnp.exp2((s - top) * EXPO)
        total = jnp.sum(p, axis=0, keepdims=True)
        out = lax.dot_general(
            v_ref[pl.ds(128 * rc, 256), :],
            p.astype(jnp.bfloat16),
            (((0,), (0,)), ((), ())),
            preferred_element_type=jnp.float32,
        )
        out = (out * ((1.0 - gate_ref[...]) / total)).astype(jnp.bfloat16)
        for x in range(X):
            o_ref[x, rc * HEAD : (rc + 1) * HEAD, :] = out[:, x * 128 : (x + 1) * 128]


def memory_kernel(count_ref, place_ref, pos_ref, gate_ref, *rest):
    q_refs = rest[: LINE + 1]
    kv_ref, o_ref, buf, stage, acc, top_s, sum_s, in_sems, out_sems = rest[LINE + 1 :]
    buf[...] = jnp.zeros(buf.shape, buf.dtype)

    def fetch(peer, rc, k):
        at = pl.multiple_of(place_ref[(peer * 2 + rc) * BLK_DEV + k], PAIR)
        return pltpu.make_async_copy(
            kv_ref.at[pl.ds(at, PAIR)], buf.at[peer % 2, rc, k], in_sems.at[peer % 2, rc, k]
        )

    def fetch_all(peer):
        for rc in range(2):
            def start(k, carry):
                fetch(peer, rc, k).start()
                return carry

            lax.fori_loop(0, count_ref[peer * 2 + rc], start, 0)

    def fetch_wait(peer):
        for rc in range(2):
            def wait(k, carry):
                fetch(peer, rc, k).wait()
                return carry

            lax.fori_loop(0, count_ref[peer * 2 + rc], wait, 0)

    def send(peer):
        to = lax.rem(pos_ref[0] + peer, LINE) * X
        return pltpu.make_async_copy(stage.at[peer % 2], o_ref.at[pl.ds(to, X)], out_sems.at[peer % 2])

    fetch_all(0)
    for peer in range(LINE):
        slot = peer % 2
        if peer + 1 < LINE:
            fetch_all(peer + 1)
        counts = [count_ref[peer * 2 + rc] for rc in range(2)]
        top_s[...] = jnp.full((2, 1, ROWS), LOWEST, jnp.float32)
        sum_s[...] = jnp.zeros((2, 1, ROWS), jnp.float32)
        acc[...] = jnp.zeros((2, HEAD, ROWS), jnp.float32)
        if peer == LINE // 2:
            sources = [(q_refs[peer], 0), (q_refs[LINE], 0)]
        else:
            q_ref = q_refs[peer]
            sources = [(q_ref, 0), (q_ref, QROWS)]
        fetch_wait(peer)

        def one_step(step, carry):
            for rc in range(2):
                q_ref, first = sources[rc]
                blocks = pl.ds(step * STEP, STEP)
                keys = buf[slot, rc, blocks, :BLOCK, :].reshape(STEP * BLOCK, HEAD)
                values = buf[slot, rc, blocks, BLOCK:, :].reshape(STEP * BLOCK, HEAD)
                s = lax.dot_general(
                    keys,
                    q_ref[first : first + ROWS, :],
                    (((1,), (1,)), ((), ())),
                    preferred_element_type=jnp.float32,
                )
                rows = lax.broadcasted_iota(jnp.int32, s.shape, 0)
                s = jnp.where(rows < (counts[rc] - step * STEP) * BLOCK, s, LOWEST)
                top = jnp.maximum(top_s[rc], jnp.max(s, axis=0, keepdims=True))
                live = (step * STEP < counts[rc]).astype(jnp.float32)
                p = jnp.exp2((s - top) * EXPO) * live
                alpha = jnp.exp2((top_s[rc] - top) * EXPO)
                sum_s[rc] = sum_s[rc] * alpha + jnp.sum(p, axis=0, keepdims=True)
                acc[rc] = acc[rc] * alpha + lax.dot_general(
                    values, p.astype(jnp.bfloat16), (((0,), (0,)), ((), ())), preferred_element_type=jnp.float32
                )
                top_s[rc] = top
            return carry

        lax.fori_loop(0, (jnp.maximum(counts[0], counts[1]) + STEP - 1) // STEP, one_step, 0)
        if peer >= 2:
            send(peer - 2).wait()
        rows = lax.broadcasted_iota(jnp.int32, (16, ROWS), 0)
        pieces = jnp.zeros((16, ROWS), jnp.float32)
        for rc in range(2):
            total = sum_s[rc]
            some = total > 0.0
            safe = jnp.where(some, total, 1.0)
            out = (acc[rc] * (gate_ref[...] / safe)).astype(jnp.bfloat16)
            level = jnp.where(some, top_s[rc] * EXPO + jnp.log2(safe), LOWEST)
            high = level.astype(jnp.bfloat16).astype(jnp.float32)
            mid = (level - high).astype(jnp.bfloat16).astype(jnp.float32)
            for i, piece in enumerate((high, mid, level - high - mid)):
                pieces = jnp.where(rows == 3 * rc + i, piece, pieces)
            for x in range(X):
                stage[slot, x, rc * HEAD : (rc + 1) * HEAD, :] = out[:, x * 128 : (x + 1) * 128]
        pieces = pieces.astype(jnp.bfloat16)
        for x in range(X):
            stage[slot, x, 2 * HEAD :, :] = pieces[:, x * 128 : (x + 1) * 128]
        send(peer).start()
    send(LINE - 2).wait()
    send(LINE - 1).wait()


def merge_kernel(core_ref, part_ref, window_ref, mine_ref, other_ref):
    first_core = core_ref[0] == 0

    def one_head(x, carry):
        flat = []
        for rc in range(2):
            levels = []
            for i in range(LINE):
                pieces = part_ref[i, x, 2 * HEAD :, :].astype(jnp.float32)
                levels.append(pieces[3 * rc : 3 * rc + 1] + pieces[3 * rc + 1 : 3 * rc + 2] + pieces[3 * rc + 2 : 3 * rc + 3])
            top = functools.reduce(jnp.maximum, levels)
            shares = [jnp.exp2(level - top) for level in levels]
            inverse = 1.0 / functools.reduce(jnp.add, shares)
            mixed = window_ref[x, rc * HEAD : (rc + 1) * HEAD, :].astype(jnp.float32)
            for i in range(LINE):
                mixed = mixed + part_ref[i, x, rc * HEAD : (rc + 1) * HEAD, :].astype(jnp.float32) * (shares[i] * inverse)
            flat.append(mixed.T)
        mine = jnp.where(first_core, flat[0], flat[1]).astype(jnp.bfloat16)
        other = jnp.where(first_core, flat[1], flat[0]).astype(jnp.bfloat16)
        for g in range(4):
            mine_ref[x * 4 + g] = mine[g * 32 : (g + 1) * 32, :]
            other_ref[x * 4 + g] = other[g * 32 : (g + 1) * 32, :]
        return carry

    lax.fori_loop(0, X, one_head, 0)


def on_device(queries, keys, values, mem_keys, mem_values, mem_ids, gate_logits):
    z, y, core = lax.axis_index("z"), lax.axis_index("y"), lax.axis_index("core")
    first_core = core == 0

    def mine_and_other(array):
        return jnp.where(first_core, array[0], array[1]), jnp.where(first_core, array[1], array[0])

    def by_core(mine, other):
        return jnp.where(first_core, mine, other), jnp.where(first_core, other, mine)

    blocks = (BLK_DEV, BLOCK, 2, HEAD)
    cache = jnp.stack([mem_keys.reshape(blocks), mem_values.reshape(blocks)])
    cache_mine, cache_other = mine_and_other(cache.transpose(3, 1, 0, 2, 4).reshape(2, SHARE, HEAD))
    q_mine, q_other = mine_and_other(
        queries.reshape(X, 32, 2, 4, HEAD).transpose(2, 0, 3, 1, 4).reshape(2, ROWS, HEAD)
    )
    ids = jnp.concatenate([mem_ids // 64, mem_ids % 64], axis=2).astype(jnp.bfloat16)
    ids = jnp.pad(ids, ((0, 0), (0, 15), (0, HEAD - 2 * TOPK)))
    ids_mine, ids_other = mine_and_other(ids)
    k_mine, k_other = mine_and_other(keys.transpose(1, 0, 2))
    v_mine, v_other = mine_and_other(values.transpose(1, 0, 2))
    swap = [(0, 1), (1, 0)]
    swapped = lax.ppermute(
        jnp.concatenate([cache_other, q_other, ids_other, k_other, v_other], axis=0), "core", swap
    )
    cache = jnp.concatenate([cache_mine, swapped[:SHARE]], axis=0)
    gathered = lax.all_gather(cache, SEQ, axis_index_groups=KV_LINES, tiled=True)
    swapped = swapped[SHARE:]

    q_list = jnp.concatenate(by_core(jnp.concatenate([q_mine, ids_mine], axis=0), swapped[:QROWS]), axis=0)
    lists = {0: q_list}
    for hop in range(1, 4):
        lists[-hop % LINE] = shift(lists[(1 - hop) % LINE], Q_LINES, 1)
        lists[hop] = shift(lists[hop - 1], Q_LINES, -1)
    lists[4] = shift(lists[5][:QROWS], Q_LINES, 1)
    lists[LINE] = shift(lists[3][QROWS:], Q_LINES, -1)
    lists = [lists[d] for d in range(LINE + 1)]

    gate = jax.nn.sigmoid(gate_logits).reshape(2, 4)
    gate = jnp.where(first_core, gate[0], gate[1])
    gate = jnp.broadcast_to(gate[None, :, None], (X, 4, 32)).reshape(1, ROWS)

    k_first, k_second = by_core(k_mine, swapped[QROWS : QROWS + 128])
    v_first, v_second = by_core(v_mine, swapped[QROWS + 128 :])
    chips = Z * Y
    onward = [(2 * i + c, 2 * i + 2 + c) for i in range(chips - 1) for c in range(2)]
    before = lax.ppermute(jnp.concatenate([k_second, v_second], axis=0), SEQ, onward)
    near_keys = jnp.concatenate([before[:128], k_first, k_second], axis=0)
    near_values = jnp.concatenate([before[128:], v_first, v_second], axis=0)
    is_first = ((z == 0) & (y == 0)).astype(jnp.int32).reshape(1)
    window = pl.pallas_call(
        window_kernel,
        out_shape=jax.ShapeDtypeStruct((X, 2 * HEAD, 128), jnp.bfloat16),
        grid_spec=pltpu.PrefetchScalarGridSpec(
            num_scalar_prefetch=1,
            grid=(1,),
            in_specs=[
                pl.BlockSpec((1, ROWS), lambda i, s: (0, 0)),
                pl.BlockSpec((2 * QROWS, HEAD), lambda i, s: (0, 0)),
                pl.BlockSpec((384, HEAD), lambda i, s: (0, 0)),
                pl.BlockSpec((384, HEAD), lambda i, s: (0, 0)),
            ],
            out_specs=pl.BlockSpec((X, 2 * HEAD, 128), lambda i, s: (0, 0, 0)),
        ),
        compiler_params=pltpu.CompilerParams(vmem_limit_bytes=24 << 20),
        cost_estimate=pl.CostEstimate(
            flops=4 * 2 * ROWS * 256 * HEAD, bytes_accessed=1 << 20, transcendentals=2 * ROWS * 256
        ),
        name="window",
    )(is_first, gate, q_list, near_keys, near_values)
    window = lax.all_to_all(window, "head", split_axis=0, concat_axis=0, tiled=True)

    coded = []
    for d in range(LINE):
        if d == LINE // 2:
            coded += [lists[d][ROWS : ROWS + 1], lists[LINE][ROWS : ROWS + 1]]
        else:
            coded += [lists[d][ROWS : ROWS + 1], lists[d][QROWS + ROWS : QROWS + ROWS + 1]]
    coded = jnp.concatenate(coded, axis=0)[:, : 2 * TOPK].astype(jnp.int32)
    wanted = coded[:, :TOPK] * 64 + coded[:, TOPK:]
    owner, local = wanted // BLK_DEV, wanted % BLK_DEV
    owner_z, owner_y, owner_core = owner // (2 * Y), (owner // 2) % Y, owner % 2
    here = jnp.where(first_core, owner_z == z, owner_y == y)
    slot = jnp.where(first_core, owner_y, owner_z) * 2 + (owner_core != core).astype(jnp.int32)
    place = slot * SHARE + local * PAIR
    rank = jnp.sum(
        (here[:, None, :] & (jnp.arange(TOPK)[None, None, :] < jnp.arange(TOPK)[None, :, None])).astype(jnp.int32),
        axis=2,
    )
    match = here[:, :, None] & (rank[:, :, None] == jnp.arange(BLK_DEV)[None, None, :])
    places = jnp.sum(jnp.where(match, place[:, :, None], 0), axis=1)
    counts = jnp.sum(here.astype(jnp.int32), axis=1)
    position = jnp.where(first_core, z, y).astype(jnp.int32).reshape(1)

    smem = pl.BlockSpec(memory_space=pltpu.SMEM)
    vmem = pl.BlockSpec(memory_space=pltpu.VMEM)
    partial = pl.pallas_call(
        memory_kernel,
        out_shape=jax.ShapeDtypeStruct((LINE * X, OROWS, 128), jnp.bfloat16),
        in_specs=[smem] * 3 + [vmem] * (LINE + 2) + [pl.BlockSpec(memory_space=pltpu.HBM)],
        out_specs=pl.BlockSpec(memory_space=pltpu.HBM),
        scratch_shapes=[
            pltpu.VMEM((2, 2, BLK_DEV, PAIR, HEAD), jnp.bfloat16),
            pltpu.VMEM((2, X, OROWS, 128), jnp.bfloat16),
            pltpu.VMEM((2, HEAD, ROWS), jnp.float32),
            pltpu.VMEM((2, 1, ROWS), jnp.float32),
            pltpu.VMEM((2, 1, ROWS), jnp.float32),
            pltpu.SemaphoreType.DMA((2, 2, BLK_DEV)),
            pltpu.SemaphoreType.DMA((2,)),
        ],
        compiler_params=pltpu.CompilerParams(vmem_limit_bytes=40 << 20),
        cost_estimate=pl.CostEstimate(
            flops=4 * 64 * ROWS * BLOCK * HEAD, bytes_accessed=6 << 20, transcendentals=64 * ROWS * BLOCK
        ),
        name="memory",
    )(counts, places.reshape(-1), position, gate, *lists, gathered)

    returned = lax.all_to_all(
        partial, SEQ + ("head",), split_axis=0, concat_axis=0, axis_index_groups=Q_PLANES, tiled=True
    ).reshape(LINE, X, OROWS, 128)
    block = pl.BlockSpec((4 * X, 32, HEAD), lambda i, s: (0, 0, 0))
    mine, other = pl.pallas_call(
        merge_kernel,
        out_shape=[jax.ShapeDtypeStruct((4 * X, 32, HEAD), jnp.bfloat16)] * 2,
        grid_spec=pltpu.PrefetchScalarGridSpec(
            num_scalar_prefetch=1,
            grid=(1,),
            in_specs=[
                pl.BlockSpec((LINE, X, OROWS, 128), lambda i, s: (0, 0, 0, 0)),
                pl.BlockSpec((X, 2 * HEAD, 128), lambda i, s: (0, 0, 0)),
            ],
            out_specs=[block, block],
        ),
        compiler_params=pltpu.CompilerParams(vmem_limit_bytes=24 << 20),
        cost_estimate=pl.CostEstimate(flops=1 << 22, bytes_accessed=4 << 20, transcendentals=1 << 13),
        name="merge",
    )(core.astype(jnp.int32).reshape(1), returned, window)
    theirs = lax.ppermute(other, "core", swap)
    heads = jnp.stack([a.reshape(X, 4, 32, HEAD) for a in by_core(mine, theirs)], axis=1)
    return heads.transpose(3, 0, 1, 2, 4).reshape(32, 8 * X * HEAD)


def solution(mesh):
    fine = Mesh(mesh.devices.reshape(Z, Y, 2, X), ("z", "y", "core", "head"))
    placed = (
        P(SEQ, "head", None),
        P(SEQ, "head", None),
        P(SEQ, "head", None),
        P(SEQ, "head", None),
        P(SEQ, "head", None),
        P("head", SEQ, None),
        P("head"),
    )
    return jax.shard_map(
        on_device, mesh=fine, in_specs=placed, out_specs=P(SEQ + ("head",), None), check_vma=False
    )
```

```python
import functools
import math

import jax
import jax.numpy as jnp
from jax import lax
from jax.experimental import pallas as pl
from jax.experimental.pallas import tpu as pltpu
from jax.sharding import Mesh
from jax.sharding import PartitionSpec as P

Z, Y, X = 8, 8, 4
LINE = 8
BLOCK = 64
TOPK = 32
BLK_DEV = 16
HEAD = 128
ROWS = 512
QROWS = ROWS + 16
PAIR = 2 * BLOCK
SHARE = BLK_DEV * PAIR
CACHE = 2 * SHARE
SHARD = CACHE + 2 * BLK_DEV + 2 * QROWS
OROWS = 2 * HEAD + 16
STEP = 4
LOWEST = -3.0e38
EXPO = HEAD**-0.5 * math.log2(math.e)
SEQ = ("z", "y", "core")


def seq_index(z, y, core):
    return (z * Y + y) * 2 + core


Y_LINES = [[[seq_index(z, y, core) for y in range(Y)] for z in range(Z)] for core in range(2)]
Z_LINES = [[[seq_index(z, y, core) for z in range(Z)] for y in range(Y)] for core in range(2)]
KV_LINES = Y_LINES[0] + Z_LINES[1]
Q_LINES = Z_LINES[0] + Y_LINES[1]


def scaled(x):
    largest = jnp.max(jnp.abs(x), axis=1, keepdims=True)
    power = 14.0 - jnp.floor(jnp.log2(jnp.maximum(largest, 1e-37)))
    power = jnp.clip(power, -113.0, 126.0)
    return (x * jnp.exp2(power)).astype(jnp.bfloat16), jnp.broadcast_to(power, x.shape).T[0:1, :]


def restored(x, power_row):
    down = jnp.broadcast_to(jnp.exp2(-power_row), (128, 128)).T
    return (x.astype(jnp.float32) * down).astype(jnp.bfloat16)


def pack_kernel(core_ref, k_ref, v_ref, q_ref, ids_ref, mine_ref, mine_powers_ref, mine_q_ref, other_ref, powers):
    core = core_ref[0]

    def cache(head, out_ref):
        def one_block(b, carry):
            at = pl.multiple_of(b * BLOCK, BLOCK)
            rows = jnp.concatenate([k_ref[head, pl.ds(at, BLOCK), :], v_ref[head, pl.ds(at, BLOCK), :]], axis=0)
            out, row = scaled(rows.astype(jnp.float32))
            out_ref[pl.ds(pl.multiple_of(b * PAIR, PAIR), PAIR), :] = out
            powers[pl.ds(b, 1), :] = row
            return carry

        lax.fori_loop(0, BLK_DEV, one_block, 0, unroll=4)
        return powers[...].astype(jnp.bfloat16)

    def queries(head, out_ref, first):
        rows = lax.broadcasted_iota(jnp.int32, (16, 128), 0)
        extra = ids_ref[head].astype(jnp.float32)
        for i in range(ROWS // 128):
            out, row = scaled(q_ref[head, i * 128 : (i + 1) * 128, :].astype(jnp.float32))
            out_ref[first + i * 128 : first + (i + 1) * 128, :] = out
            extra = jnp.where(rows == i, row, extra)
        out_ref[first + ROWS : first + QROWS, :] = extra.astype(jnp.bfloat16)

    mine_powers_ref[...] = cache(core, mine_ref)
    other_ref[SHARE : SHARE + BLK_DEV, :] = cache(1 - core, other_ref)
    queries(1 - core, mine_q_ref, 0)
    queries(core, other_ref, SHARE + BLK_DEV)


def window_kernel(first_ref, q_ref, k_ref, v_ref, o_ref):
    for rc in range(2):
        s = lax.dot_general(
            k_ref[pl.ds(128 * rc, 256), :],
            q_ref[rc],
            (((1,), (1,)), ((), ())),
            preferred_element_type=jnp.float32,
        )
        kpos = lax.broadcasted_iota(jnp.int32, s.shape, 0) - 128
        qpos = lax.broadcasted_iota(jnp.int32, s.shape, 1) & 127
        allowed = (kpos <= qpos) & (kpos > qpos - 128)
        if rc == 0:
            allowed = allowed & ((kpos >= 0) | (first_ref[0] == 0))
        s = jnp.where(allowed, s, LOWEST)
        top = jnp.max(s, axis=0, keepdims=True)
        p = jnp.exp2((s - top) * EXPO)
        total = jnp.sum(p, axis=0, keepdims=True)
        out = lax.dot_general(
            v_ref[pl.ds(128 * rc, 256), :],
            p.astype(jnp.bfloat16),
            (((0,), (0,)), ((), ())),
            preferred_element_type=jnp.float32,
        )
        o_ref[rc] = out / total


def memory_kernel(count_ref, place_ref, power_at_ref, q_ref, powers_ref, kv_ref, o_ref, buf, stage, q_buf, acc, top_s, sum_s, in_sems, out_sems):
    buf[...] = jnp.zeros(buf.shape, buf.dtype)

    def fetch(peer, rc, k):
        at = pl.multiple_of(place_ref[(peer * 2 + rc) * BLK_DEV + k], 16)
        return pltpu.make_async_copy(
            kv_ref.at[pl.ds(at, PAIR)], buf.at[peer % 2, rc, k], in_sems.at[peer % 2, rc, k]
        )

    def fetch_all(peer):
        for rc in range(2):
            def start(k, carry):
                fetch(peer, rc, k).start()
                return carry

            lax.fori_loop(0, count_ref[peer * 2 + rc], start, 0)

    def fetch_wait(peer):
        for rc in range(2):
            def wait(k, carry):
                fetch(peer, rc, k).wait()
                return carry

            lax.fori_loop(0, count_ref[peer * 2 + rc], wait, 0)

    def send(peer):
        return pltpu.make_async_copy(stage.at[peer % 2], o_ref.at[peer], out_sems.at[peer % 2])

    fetch_all(0)
    for peer in range(LINE):
        slot = peer % 2
        if peer + 1 < LINE:
            fetch_all(peer + 1)
        counts = [count_ref[peer * 2 + rc] for rc in range(2)]
        top_s[...] = jnp.full((2, 1, ROWS), LOWEST, jnp.float32)
        sum_s[...] = jnp.zeros((2, 1, ROWS), jnp.float32)
        acc[...] = jnp.zeros((2, HEAD, ROWS), jnp.float32)
        for rc in range(2):
            first = (peer * 2 + rc) * QROWS
            extra = q_ref[first + ROWS : first + QROWS, :].astype(jnp.float32)
            for i in range(ROWS // 128):
                q_buf[rc, i * 128 : (i + 1) * 128, :] = restored(
                    q_ref[first + i * 128 : first + (i + 1) * 128, :], extra[i : i + 1, :]
                )
        fetch_wait(peer)

        def one_step(step, carry):
            for rc in range(2):
                pairs = []
                for i in range(STEP):
                    at = power_at_ref[(peer * 2 + rc) * BLK_DEV + step * STEP + i]
                    pairs.append(restored(buf[slot, rc, step * STEP + i], powers_ref[pl.ds(at, 1), :]))
                keys = jnp.concatenate([pair[:BLOCK] for pair in pairs], axis=0)
                values = jnp.concatenate([pair[BLOCK:] for pair in pairs], axis=0)
                s = lax.dot_general(
                    keys, q_buf[rc], (((1,), (1,)), ((), ())), preferred_element_type=jnp.float32
                )
                rows = lax.broadcasted_iota(jnp.int32, s.shape, 0)
                s = jnp.where(rows < (counts[rc] - step * STEP) * BLOCK, s, LOWEST)
                top = jnp.maximum(top_s[rc], jnp.max(s, axis=0, keepdims=True))
                live = (step * STEP < counts[rc]).astype(jnp.float32)
                p = jnp.exp2((s - top) * EXPO) * live
                alpha = jnp.exp2((top_s[rc] - top) * EXPO)
                sum_s[rc] = sum_s[rc] * alpha + jnp.sum(p, axis=0, keepdims=True)
                acc[rc] = acc[rc] * alpha + lax.dot_general(
                    values, p.astype(jnp.bfloat16), (((0,), (0,)), ((), ())), preferred_element_type=jnp.float32
                )
                top_s[rc] = top
            return carry

        lax.fori_loop(0, (jnp.maximum(counts[0], counts[1]) + STEP - 1) // STEP, one_step, 0)
        if peer >= 2:
            send(peer - 2).wait()
        rows = lax.broadcasted_iota(jnp.int32, (16, ROWS), 0)
        pieces = jnp.zeros((16, ROWS), jnp.float32)
        for rc in range(2):
            total = sum_s[rc]
            some = total > 0.0
            safe = jnp.where(some, total, 1.0)
            stage[slot, rc * HEAD : (rc + 1) * HEAD, :] = (acc[rc] / safe).astype(jnp.bfloat16)
            level = jnp.where(some, top_s[rc] * EXPO + jnp.log2(safe), LOWEST)
            high = level.astype(jnp.bfloat16).astype(jnp.float32)
            mid = (level - high).astype(jnp.bfloat16).astype(jnp.float32)
            for i, piece in enumerate((high, mid, level - high - mid)):
                pieces = jnp.where(rows == 3 * rc + i, piece, pieces)
        stage[slot, 2 * HEAD :, :] = pieces.astype(jnp.bfloat16)
        send(peer).start()
    send(LINE - 2).wait()
    send(LINE - 1).wait()


def merge_kernel(part_ref, window_ref, gate_ref, o_ref):
    gate = gate_ref[...]
    for rc in range(2):
        levels = []
        for i in range(LINE):
            pieces = part_ref[i, 2 * HEAD :, :].astype(jnp.float32)[3 * rc : 3 * rc + 3, :]
            levels.append(pieces[0:1] + pieces[1:2] + pieces[2:3])
        top = functools.reduce(jnp.maximum, levels)
        shares = [jnp.exp2(level - top) for level in levels]
        scale = gate / functools.reduce(jnp.add, shares)
        mixed = (1.0 - gate) * window_ref[rc]
        for i in range(LINE):
            mixed = mixed + part_ref[i, rc * HEAD : (rc + 1) * HEAD, :].astype(jnp.float32) * (shares[i] * scale)
        for g in range(4):
            flat = mixed[:, g * 128 : (g + 1) * 128].T.astype(jnp.bfloat16)
            for x in range(X):
                o_ref[x * 2 + rc, :, g * 128 : (g + 1) * 128] = flat[x * 32 : (x + 1) * 32, :]


def on_device(queries, keys, values, mem_keys, mem_values, mem_ids, gate_logits):
    z, y, core = lax.axis_index("z"), lax.axis_index("y"), lax.axis_index("core")
    first_core = core == 0
    smem = pl.BlockSpec(memory_space=pltpu.SMEM)
    vmem = pl.BlockSpec(memory_space=pltpu.VMEM)
    swap = [(0, 1), (1, 0)]

    def mine_and_other(array):
        return jnp.where(first_core, array[0], array[1]), jnp.where(first_core, array[1], array[0])

    def by_core(mine, other):
        return jnp.where(first_core, mine, other), jnp.where(first_core, other, mine)

    by_head = queries.reshape(128, 2, 4, HEAD).transpose(1, 2, 0, 3).reshape(2, ROWS, HEAD)
    ids = jnp.concatenate([mem_ids // 64, mem_ids % 64], axis=2).astype(jnp.bfloat16)
    ids = jnp.pad(ids, ((0, 0), (4, 11), (0, HEAD - 2 * TOPK)))
    mine, mine_powers, mine_q, other = pl.pallas_call(
        pack_kernel,
        out_shape=[
            jax.ShapeDtypeStruct((SHARE, HEAD), jnp.bfloat16),
            jax.ShapeDtypeStruct((BLK_DEV, HEAD), jnp.bfloat16),
            jax.ShapeDtypeStruct((QROWS, HEAD), jnp.bfloat16),
            jax.ShapeDtypeStruct((SHARE + BLK_DEV + QROWS, HEAD), jnp.bfloat16),
        ],
        in_specs=[smem] + [vmem] * 4,
        out_specs=[vmem] * 4,
        scratch_shapes=[pltpu.VMEM((BLK_DEV, HEAD), jnp.float32)],
        compiler_params=pltpu.CompilerParams(vmem_limit_bytes=16 << 20),
        cost_estimate=pl.CostEstimate(flops=1 << 22, bytes_accessed=3 << 20, transcendentals=1 << 13),
        name="pack",
    )(
        core.astype(jnp.int32).reshape(1),
        mem_keys.transpose(1, 0, 2),
        mem_values.transpose(1, 0, 2),
        by_head,
        ids,
    )
    theirs = lax.ppermute(other, "core", swap)
    their_cache, their_powers, their_q = jnp.split(theirs, [SHARE, SHARE + BLK_DEV])
    shard = jnp.concatenate(
        [mine, their_cache, mine_powers, their_powers, *by_core(mine_q, their_q)], axis=0
    ).astype(jnp.float16)
    gathered = lax.all_gather(shard, SEQ, axis_index_groups=KV_LINES, tiled=True)
    parts = gathered.reshape(LINE, SHARD, HEAD)
    lists = lax.ppermute(parts[:, SHARD - 2 * QROWS :], "core", swap)
    lists = lists.reshape(2 * LINE * QROWS, HEAD).astype(jnp.bfloat16)
    cache = gathered.astype(jnp.bfloat16)
    powers = parts[:, CACHE : CACHE + 2 * BLK_DEV].reshape(2 * LINE * BLK_DEV, HEAD).astype(jnp.float32)

    coded = lists.reshape(2 * LINE, QROWS, HEAD)[:, ROWS + 4, : 2 * TOPK].astype(jnp.int32)
    wanted = coded[:, :TOPK] * 64 + coded[:, TOPK:]
    owner, local = wanted // BLK_DEV, wanted % BLK_DEV
    owner_z, owner_y, owner_core = owner // (2 * Y), (owner // 2) % Y, owner % 2
    here = jnp.where(first_core, owner_z == z, owner_y == y)
    position = jnp.where(first_core, owner_y, owner_z)
    index = (position * 2 + (owner_core != core).astype(jnp.int32)) * BLK_DEV + local
    rank = jnp.sum(
        (here[:, None, :] & (jnp.arange(TOPK)[None, None, :] < jnp.arange(TOPK)[None, :, None])).astype(jnp.int32),
        axis=2,
    )
    match = here[:, :, None] & (rank[:, :, None] == jnp.arange(BLK_DEV)[None, None, :])
    indices = jnp.sum(jnp.where(match, index[:, :, None], 0), axis=1).reshape(-1)
    places = (indices // (2 * BLK_DEV)) * SHARD + (indices % (2 * BLK_DEV)) * PAIR
    counts = jnp.sum(here.astype(jnp.int32), axis=1)

    partial = pl.pallas_call(
        memory_kernel,
        out_shape=jax.ShapeDtypeStruct((LINE, OROWS, ROWS), jnp.bfloat16),
        in_specs=[smem] * 3 + [vmem] * 2 + [pl.BlockSpec(memory_space=pltpu.HBM)],
        out_specs=pl.BlockSpec(memory_space=pltpu.HBM),
        scratch_shapes=[
            pltpu.VMEM((2, 2, BLK_DEV, PAIR, HEAD), jnp.bfloat16),
            pltpu.VMEM((2, OROWS, ROWS), jnp.bfloat16),
            pltpu.VMEM((2, ROWS, HEAD), jnp.bfloat16),
            pltpu.VMEM((2, HEAD, ROWS), jnp.float32),
            pltpu.VMEM((2, 1, ROWS), jnp.float32),
            pltpu.VMEM((2, 1, ROWS), jnp.float32),
            pltpu.SemaphoreType.DMA((2, 2, BLK_DEV)),
            pltpu.SemaphoreType.DMA((2,)),
        ],
        compiler_params=pltpu.CompilerParams(vmem_limit_bytes=24 << 20),
        cost_estimate=pl.CostEstimate(
            flops=4 * 64 * ROWS * BLOCK * HEAD, bytes_accessed=6 << 20, transcendentals=64 * ROWS * BLOCK
        ),
        name="memory",
    )(counts, places, indices, lists, powers, cache)
    returned = lax.all_to_all(
        partial, SEQ, split_axis=0, concat_axis=0, axis_index_groups=Q_LINES, tiled=True
    )

    q_mine, q_other = mine_and_other(by_head)
    k_mine, k_other = mine_and_other(keys.transpose(1, 0, 2))
    v_mine, v_other = mine_and_other(values.transpose(1, 0, 2))
    near = lax.ppermute(jnp.concatenate([q_other, k_other, v_other], axis=0), "core", swap)
    q_first, q_second = by_core(q_mine, near[:ROWS])
    k_first, k_second = by_core(k_mine, near[ROWS : ROWS + 128])
    v_first, v_second = by_core(v_mine, near[ROWS + 128 :])
    onward = [(2 * i + c, 2 * i + 2 + c) for i in range(Z * Y - 1) for c in range(2)]
    before = lax.ppermute(jnp.concatenate([k_second, v_second], axis=0), SEQ, onward)
    is_first = ((z == 0) & (y == 0)).astype(jnp.int32).reshape(1)
    window = pl.pallas_call(
        window_kernel,
        out_shape=jax.ShapeDtypeStruct((2, HEAD, ROWS), jnp.float32),
        in_specs=[smem] + [vmem] * 3,
        out_specs=vmem,
        compiler_params=pltpu.CompilerParams(vmem_limit_bytes=16 << 20),
        cost_estimate=pl.CostEstimate(
            flops=4 * 2 * ROWS * 256 * HEAD, bytes_accessed=1 << 20, transcendentals=2 * ROWS * 256
        ),
        name="window",
    )(
        is_first,
        jnp.stack([q_first, q_second]),
        jnp.concatenate([before[:128], k_first, k_second], axis=0),
        jnp.concatenate([before[128:], v_first, v_second], axis=0),
    )

    gate = jax.nn.sigmoid(gate_logits).reshape(2, 4)
    gate = jnp.repeat(jnp.where(first_core, gate[0], gate[1]), 128)[None, :]
    mixed = pl.pallas_call(
        merge_kernel,
        out_shape=jax.ShapeDtypeStruct((2 * X, 32, ROWS), jnp.bfloat16),
        in_specs=[vmem] * 3,
        out_specs=vmem,
        compiler_params=pltpu.CompilerParams(vmem_limit_bytes=16 << 20),
        cost_estimate=pl.CostEstimate(flops=1 << 22, bytes_accessed=4 << 20, transcendentals=1 << 13),
        name="merge",
    )(returned, window, gate)
    rows = lax.all_to_all(mixed, ("head", "core"), split_axis=0, concat_axis=0, tiled=True)
    return rows.transpose(1, 0, 2).reshape(32, 2 * X * ROWS)


def solution(mesh):
    fine = Mesh(mesh.devices.reshape(Z, Y, 2, X), ("z", "y", "core", "head"))
    placed = (
        P(SEQ, "head", None),
        P(SEQ, "head", None),
        P(SEQ, "head", None),
        P(SEQ, "head", None),
        P(SEQ, "head", None),
        P("head", SEQ, None),
        P("head"),
    )
    return jax.shard_map(
        on_device, mesh=fine, in_specs=placed, out_specs=P(SEQ + ("head",), None), check_vma=False
    )
```

```python
import functools
import math

import jax
import jax.numpy as jnp
from jax import lax
from jax.experimental import pallas as pl
from jax.experimental.pallas import tpu as pltpu
from jax.sharding import Mesh
from jax.sharding import PartitionSpec as P

Z, Y, X = 8, 8, 4
LINE = 8
BLOCK = 64
TOPK = 32
BLK_DEV = 16
HEAD = 128
ROWS = 512
QROWS = ROWS + 16
PAIR = 2 * BLOCK
SHARE = BLK_DEV * PAIR
CACHE = 2 * SHARE
SHARD = CACHE + 2 * BLK_DEV + 2 * QROWS
OROWS = 2 * HEAD + 16
STEP = 4
LOWEST = -3.0e38
EXPO = HEAD**-0.5 * math.log2(math.e)
SEQ = ("z", "y", "core")


def seq_index(z, y, core):
    return (z * Y + y) * 2 + core


Y_LINES = [[[seq_index(z, y, core) for y in range(Y)] for z in range(Z)] for core in range(2)]
Z_LINES = [[[seq_index(z, y, core) for z in range(Z)] for y in range(Y)] for core in range(2)]
KV_LINES = Y_LINES[0] + Z_LINES[1]
Q_LINES = Z_LINES[0] + Y_LINES[1]


def scaled(x):
    largest = jnp.max(jnp.abs(x), axis=1, keepdims=True)
    power = 14.0 - jnp.floor(jnp.log2(jnp.maximum(largest, 1e-37)))
    power = jnp.clip(power, -113.0, 126.0)
    return (x * jnp.exp2(power)).astype(jnp.bfloat16), jnp.broadcast_to(power, x.shape).T[0:1, :]


def restored(x, power_row):
    down = jnp.broadcast_to(jnp.exp2(-power_row), (128, 128)).T
    return (x.astype(jnp.float32) * down).astype(jnp.bfloat16)


def pack_kernel(
    where_ref, k_ref, v_ref, q_ref, ids_ref, mine_ref, mine_powers_ref, mine_q_ref, other_ref, place_ref, powers
):
    for i in range(3):
        place_ref[i : i + 1, :] = jnp.full((1, 128), where_ref[i], jnp.int32)
    core = where_ref[2]

    def cache(head, out_ref):
        def one_block(b, carry):
            at = pl.multiple_of(b * BLOCK, BLOCK)
            rows = jnp.concatenate([k_ref[head, pl.ds(at, BLOCK), :], v_ref[head, pl.ds(at, BLOCK), :]], axis=0)
            out, row = scaled(rows.astype(jnp.float32))
            out_ref[pl.ds(pl.multiple_of(b * PAIR, PAIR), PAIR), :] = out
            powers[pl.ds(b, 1), :] = row
            return carry

        lax.fori_loop(0, BLK_DEV, one_block, 0, unroll=4)
        return powers[...].astype(jnp.bfloat16)

    def queries(head, out_ref, first):
        rows = lax.broadcasted_iota(jnp.int32, (16, 128), 0)
        extra = ids_ref[head].astype(jnp.float32)
        for i in range(ROWS // 128):
            out, row = scaled(q_ref[head, i * 128 : (i + 1) * 128, :].astype(jnp.float32))
            out_ref[first + i * 128 : first + (i + 1) * 128, :] = out
            extra = jnp.where(rows == i, row, extra)
        out_ref[first + ROWS : first + QROWS, :] = extra.astype(jnp.bfloat16)

    mine_powers_ref[...] = cache(core, mine_ref)
    other_ref[SHARE : SHARE + BLK_DEV, :] = cache(1 - core, other_ref)
    queries(1 - core, mine_q_ref, 0)
    queries(core, other_ref, SHARE + BLK_DEV)


def window_kernel(first_ref, q_ref, k_ref, v_ref, o_ref):
    for rc in range(2):
        s = lax.dot_general(
            k_ref[pl.ds(128 * rc, 256), :],
            q_ref[rc],
            (((1,), (1,)), ((), ())),
            preferred_element_type=jnp.float32,
        )
        kpos = lax.broadcasted_iota(jnp.int32, s.shape, 0) - 128
        qpos = lax.broadcasted_iota(jnp.int32, s.shape, 1) & 127
        allowed = (kpos <= qpos) & (kpos > qpos - 128)
        if rc == 0:
            allowed = allowed & ((kpos >= 0) | (first_ref[0] == 0))
        s = jnp.where(allowed, s, LOWEST)
        top = jnp.max(s, axis=0, keepdims=True)
        p = jnp.exp2((s - top) * EXPO)
        total = jnp.sum(p, axis=0, keepdims=True)
        out = lax.dot_general(
            v_ref[pl.ds(128 * rc, 256), :],
            p.astype(jnp.bfloat16),
            (((0,), (0,)), ((), ())),
            preferred_element_type=jnp.float32,
        )
        o_ref[rc] = out / total


def memory_kernel(count_ref, place_ref, power_at_ref, q_ref, powers_ref, kv_ref, o_ref, buf, stage, q_buf, acc, top_s, sum_s, in_sems, out_sems):
    buf[...] = jnp.zeros(buf.shape, buf.dtype)

    def fetch(peer, rc, k):
        at = pl.multiple_of(place_ref[peer * 2 + rc, k], 16)
        return pltpu.make_async_copy(
            kv_ref.at[pl.ds(at, PAIR)], buf.at[peer % 2, rc, k], in_sems.at[peer % 2, rc, k]
        )

    def fetch_all(peer):
        for rc in range(2):
            def start(k, carry):
                fetch(peer, rc, k).start()
                return carry

            lax.fori_loop(0, count_ref[peer * 2 + rc], start, 0)

    def fetch_wait(peer):
        for rc in range(2):
            def wait(k, carry):
                fetch(peer, rc, k).wait()
                return carry

            lax.fori_loop(0, count_ref[peer * 2 + rc], wait, 0)

    def send(peer):
        return pltpu.make_async_copy(stage.at[peer % 2], o_ref.at[peer], out_sems.at[peer % 2])

    fetch_all(0)
    for peer in range(LINE):
        slot = peer % 2
        if peer + 1 < LINE:
            fetch_all(peer + 1)
        counts = [count_ref[peer * 2 + rc] for rc in range(2)]
        top_s[...] = jnp.full((2, 1, ROWS), LOWEST, jnp.float32)
        sum_s[...] = jnp.zeros((2, 1, ROWS), jnp.float32)
        acc[...] = jnp.zeros((2, HEAD, ROWS), jnp.float32)
        for rc in range(2):
            first = (peer * 2 + rc) * QROWS
            extra = q_ref[first + ROWS : first + QROWS, :].astype(jnp.float32)
            for i in range(ROWS // 128):
                q_buf[rc, i * 128 : (i + 1) * 128, :] = restored(
                    q_ref[first + i * 128 : first + (i + 1) * 128, :], extra[i : i + 1, :]
                )
        fetch_wait(peer)

        def one_step(step, carry):
            for rc in range(2):
                pairs = []
                for i in range(STEP):
                    at = power_at_ref[peer * 2 + rc, step * STEP + i]
                    pairs.append(restored(buf[slot, rc, step * STEP + i], powers_ref[pl.ds(at, 1), :]))
                keys = jnp.concatenate([pair[:BLOCK] for pair in pairs], axis=0)
                values = jnp.concatenate([pair[BLOCK:] for pair in pairs], axis=0)
                s = lax.dot_general(
                    keys, q_buf[rc], (((1,), (1,)), ((), ())), preferred_element_type=jnp.float32
                )
                rows = lax.broadcasted_iota(jnp.int32, s.shape, 0)
                s = jnp.where(rows < (counts[rc] - step * STEP) * BLOCK, s, LOWEST)
                top = jnp.maximum(top_s[rc], jnp.max(s, axis=0, keepdims=True))
                live = (step * STEP < counts[rc]).astype(jnp.float32)
                p = jnp.exp2((s - top) * EXPO) * live
                alpha = jnp.exp2((top_s[rc] - top) * EXPO)
                sum_s[rc] = sum_s[rc] * alpha + jnp.sum(p, axis=0, keepdims=True)
                acc[rc] = acc[rc] * alpha + lax.dot_general(
                    values, p.astype(jnp.bfloat16), (((0,), (0,)), ((), ())), preferred_element_type=jnp.float32
                )
                top_s[rc] = top
            return carry

        lax.fori_loop(0, (jnp.maximum(counts[0], counts[1]) + STEP - 1) // STEP, one_step, 0)
        if peer >= 2:
            send(peer - 2).wait()
        rows = lax.broadcasted_iota(jnp.int32, (16, ROWS), 0)
        pieces = jnp.zeros((16, ROWS), jnp.float32)
        for rc in range(2):
            total = sum_s[rc]
            some = total > 0.0
            safe = jnp.where(some, total, 1.0)
            stage[slot, rc * HEAD : (rc + 1) * HEAD, :] = (acc[rc] / safe).astype(jnp.bfloat16)
            level = jnp.where(some, top_s[rc] * EXPO + jnp.log2(safe), LOWEST)
            high = level.astype(jnp.bfloat16).astype(jnp.float32)
            mid = (level - high).astype(jnp.bfloat16).astype(jnp.float32)
            for i, piece in enumerate((high, mid, level - high - mid)):
                pieces = jnp.where(rows == 3 * rc + i, piece, pieces)
        stage[slot, 2 * HEAD :, :] = pieces.astype(jnp.bfloat16)
        send(peer).start()
    send(LINE - 2).wait()
    send(LINE - 1).wait()


def merge_kernel(part_ref, window_ref, gate_ref, o_ref):
    gate = gate_ref[...]
    for rc in range(2):
        levels = []
        for i in range(LINE):
            pieces = part_ref[i, 2 * HEAD :, :].astype(jnp.float32)[3 * rc : 3 * rc + 3, :]
            levels.append(pieces[0:1] + pieces[1:2] + pieces[2:3])
        top = functools.reduce(jnp.maximum, levels)
        shares = [jnp.exp2(level - top) for level in levels]
        scale = gate / functools.reduce(jnp.add, shares)
        mixed = (1.0 - gate) * window_ref[rc]
        for i in range(LINE):
            mixed = mixed + part_ref[i, rc * HEAD : (rc + 1) * HEAD, :].astype(jnp.float32) * (shares[i] * scale)
        for g in range(4):
            flat = mixed[:, g * 128 : (g + 1) * 128].T.astype(jnp.bfloat16)
            for x in range(X):
                o_ref[x * 2 + rc, :, g * 128 : (g + 1) * 128] = flat[x * 32 : (x + 1) * 32, :]


def on_device(queries, keys, values, mem_keys, mem_values, mem_ids, gate_logits):
    z, y, core = lax.axis_index("z"), lax.axis_index("y"), lax.axis_index("core")
    first_core = core == 0
    smem = pl.BlockSpec(memory_space=pltpu.SMEM)
    vmem = pl.BlockSpec(memory_space=pltpu.VMEM)
    swap = [(0, 1), (1, 0)]

    def mine_and_other(array):
        return jnp.where(first_core, array[0], array[1]), jnp.where(first_core, array[1], array[0])

    def by_core(mine, other):
        return jnp.where(first_core, mine, other), jnp.where(first_core, other, mine)

    by_head = queries.reshape(128, 2, 4, HEAD).transpose(1, 2, 0, 3).reshape(2, ROWS, HEAD)
    ids = jnp.concatenate([mem_ids // 64, mem_ids % 64], axis=2).astype(jnp.bfloat16)
    ids = jnp.pad(ids, ((0, 0), (4, 11), (0, HEAD - 2 * TOPK)))
    mine, mine_powers, mine_q, other, placed = pl.pallas_call(
        pack_kernel,
        out_shape=[
            jax.ShapeDtypeStruct((SHARE, HEAD), jnp.bfloat16),
            jax.ShapeDtypeStruct((BLK_DEV, HEAD), jnp.bfloat16),
            jax.ShapeDtypeStruct((QROWS, HEAD), jnp.bfloat16),
            jax.ShapeDtypeStruct((SHARE + BLK_DEV + QROWS, HEAD), jnp.bfloat16),
            jax.ShapeDtypeStruct((8, 128), jnp.int32),
        ],
        in_specs=[smem] + [vmem] * 4,
        out_specs=[vmem] * 5,
        scratch_shapes=[pltpu.VMEM((BLK_DEV, HEAD), jnp.float32)],
        compiler_params=pltpu.CompilerParams(vmem_limit_bytes=16 << 20),
        cost_estimate=pl.CostEstimate(flops=1 << 22, bytes_accessed=3 << 20, transcendentals=1 << 13),
        name="pack",
    )(
        jnp.stack([z, y, core]).astype(jnp.int32),
        mem_keys.transpose(1, 0, 2),
        mem_values.transpose(1, 0, 2),
        by_head,
        ids,
    )
    theirs = lax.ppermute(other, "core", swap)
    their_cache, their_powers, their_q = jnp.split(theirs, [SHARE, SHARE + BLK_DEV])
    shard = jnp.concatenate(
        [mine, their_cache, mine_powers, their_powers, *by_core(mine_q, their_q)], axis=0
    ).astype(jnp.float16)
    gathered = lax.all_gather(shard, SEQ, axis_index_groups=KV_LINES, tiled=True)
    parts = gathered.reshape(LINE, SHARD, HEAD)
    lists = lax.ppermute(parts[:, SHARD - 2 * QROWS :], "core", swap)
    lists = lists.reshape(2 * LINE * QROWS, HEAD).astype(jnp.bfloat16)
    cache = gathered.astype(jnp.bfloat16)
    powers = parts[:, CACHE : CACHE + 2 * BLK_DEV].reshape(2 * LINE * BLK_DEV, HEAD).astype(jnp.float32)

    coded = lists.reshape(2 * LINE, QROWS, HEAD)[:, ROWS + 4, : 2 * TOPK].astype(jnp.int32)
    wanted = coded[:, :TOPK] * 64 + coded[:, TOPK:]
    owner, local = wanted // BLK_DEV, wanted % BLK_DEV
    owner_z, owner_y, owner_core = owner // (2 * Y), (owner // 2) % Y, owner % 2
    my_z, my_y, my_core = (placed[i : i + 1, :TOPK] for i in range(3))
    here = jnp.where(my_core == 0, owner_z == my_z, owner_y == my_y)
    position = jnp.where(my_core == 0, owner_y, owner_z)
    index = (position * 2 + (owner_core != my_core).astype(jnp.int32)) * BLK_DEV + local
    rank = jnp.sum(
        (here[:, None, :] & (jnp.arange(TOPK)[None, None, :] < jnp.arange(TOPK)[None, :, None])).astype(jnp.int32),
        axis=2,
    )
    match = here[:, :, None] & (rank[:, :, None] == jnp.arange(BLK_DEV)[None, None, :])
    indices = jnp.sum(jnp.where(match, index[:, :, None], 0), axis=1)
    places = (indices // (2 * BLK_DEV)) * SHARD + (indices % (2 * BLK_DEV)) * PAIR
    counts = jnp.sum(here.astype(jnp.int32), axis=1)

    partial = pl.pallas_call(
        memory_kernel,
        out_shape=jax.ShapeDtypeStruct((LINE, OROWS, ROWS), jnp.bfloat16),
        in_specs=[smem] * 3 + [vmem] * 2 + [pl.BlockSpec(memory_space=pltpu.HBM)],
        out_specs=pl.BlockSpec(memory_space=pltpu.HBM),
        scratch_shapes=[
            pltpu.VMEM((2, 2, BLK_DEV, PAIR, HEAD), jnp.bfloat16),
            pltpu.VMEM((2, OROWS, ROWS), jnp.bfloat16),
            pltpu.VMEM((2, ROWS, HEAD), jnp.bfloat16),
            pltpu.VMEM((2, HEAD, ROWS), jnp.float32),
            pltpu.VMEM((2, 1, ROWS), jnp.float32),
            pltpu.VMEM((2, 1, ROWS), jnp.float32),
            pltpu.SemaphoreType.DMA((2, 2, BLK_DEV)),
            pltpu.SemaphoreType.DMA((2,)),
        ],
        compiler_params=pltpu.CompilerParams(vmem_limit_bytes=24 << 20),
        cost_estimate=pl.CostEstimate(
            flops=4 * 64 * ROWS * BLOCK * HEAD, bytes_accessed=6 << 20, transcendentals=64 * ROWS * BLOCK
        ),
        name="memory",
    )(counts, places, indices, lists, powers, cache)
    returned = lax.all_to_all(
        partial, SEQ, split_axis=0, concat_axis=0, axis_index_groups=Q_LINES, tiled=True
    )

    q_mine, q_other = mine_and_other(by_head)
    k_mine, k_other = mine_and_other(keys.transpose(1, 0, 2))
    v_mine, v_other = mine_and_other(values.transpose(1, 0, 2))
    near = lax.ppermute(jnp.concatenate([q_other, k_other, v_other], axis=0), "core", swap)
    q_first, q_second = by_core(q_mine, near[:ROWS])
    k_first, k_second = by_core(k_mine, near[ROWS : ROWS + 128])
    v_first, v_second = by_core(v_mine, near[ROWS + 128 :])
    onward = [(2 * i + c, 2 * i + 2 + c) for i in range(Z * Y - 1) for c in range(2)]
    before = lax.ppermute(jnp.concatenate([k_second, v_second], axis=0), SEQ, onward)
    is_first = ((z == 0) & (y == 0)).astype(jnp.int32).reshape(1)
    window = pl.pallas_call(
        window_kernel,
        out_shape=jax.ShapeDtypeStruct((2, HEAD, ROWS), jnp.float32),
        in_specs=[smem] + [vmem] * 3,
        out_specs=vmem,
        compiler_params=pltpu.CompilerParams(vmem_limit_bytes=16 << 20),
        cost_estimate=pl.CostEstimate(
            flops=4 * 2 * ROWS * 256 * HEAD, bytes_accessed=1 << 20, transcendentals=2 * ROWS * 256
        ),
        name="window",
    )(
        is_first,
        jnp.stack([q_first, q_second]),
        jnp.concatenate([before[:128], k_first, k_second], axis=0),
        jnp.concatenate([before[128:], v_first, v_second], axis=0),
    )

    gate = jax.nn.sigmoid(gate_logits).reshape(2, 4)
    gate = jnp.repeat(jnp.where(first_core, gate[0], gate[1]), 128)[None, :]
    mixed = pl.pallas_call(
        merge_kernel,
        out_shape=jax.ShapeDtypeStruct((2 * X, 32, ROWS), jnp.bfloat16),
        in_specs=[vmem] * 3,
        out_specs=vmem,
        compiler_params=pltpu.CompilerParams(vmem_limit_bytes=16 << 20),
        cost_estimate=pl.CostEstimate(flops=1 << 22, bytes_accessed=4 << 20, transcendentals=1 << 13),
        name="merge",
    )(returned, window, gate)
    rows = lax.all_to_all(mixed, ("head", "core"), split_axis=0, concat_axis=0, tiled=True)
    return rows.transpose(1, 0, 2).reshape(32, 2 * X * ROWS)


def solution(mesh):
    fine = Mesh(mesh.devices.reshape(Z, Y, 2, X), ("z", "y", "core", "head"))
    placed = (
        P(SEQ, "head", None),
        P(SEQ, "head", None),
        P(SEQ, "head", None),
        P(SEQ, "head", None),
        P(SEQ, "head", None),
        P("head", SEQ, None),
        P("head"),
    )
    return jax.shard_map(
        on_device, mesh=fine, in_specs=placed, out_specs=P(SEQ + ("head",), None), check_vma=False
    )
```

```python
import functools
import math

import jax
import jax.numpy as jnp
from jax import lax
from jax.experimental import pallas as pl
from jax.experimental.pallas import tpu as pltpu
from jax.sharding import Mesh
from jax.sharding import PartitionSpec as P

Z, Y, X = 8, 8, 4
LINE = 8
BLOCK = 64
TOPK = 32
BLK_DEV = 16
HEAD = 128
ROWS = 512
QROWS = ROWS + 16
PAIR = 2 * BLOCK
SHARE = BLK_DEV * PAIR
CACHE = 2 * SHARE
SHARD = CACHE + 2 * BLK_DEV + 2 * QROWS
OROWS = 2 * HEAD + 16
STEP = 8
LOWEST = -3.0e38
WAVES = ((4, 3, 5), (2, 6), (1, 7, 0))
EXPO = HEAD**-0.5 * math.log2(math.e)
SEQ = ("z", "y", "core")


def seq_index(z, y, core):
    return (z * Y + y) * 2 + core


Y_LINES = [[[seq_index(z, y, core) for y in range(Y)] for z in range(Z)] for core in range(2)]
Z_LINES = [[[seq_index(z, y, core) for z in range(Z)] for y in range(Y)] for core in range(2)]
KV_LINES = Y_LINES[0] + Z_LINES[1]
Q_LINES = Z_LINES[0] + Y_LINES[1]


def shift(value, lines, by):
    return lax.ppermute(value, SEQ, [(line[i], line[(i + by) % LINE]) for line in lines for i in range(LINE)])


def scaled(x):
    largest = jnp.max(jnp.abs(x), axis=1, keepdims=True)
    power = 14.0 - jnp.floor(jnp.log2(jnp.maximum(largest, 1e-37)))
    power = jnp.clip(power, -113.0, 126.0)
    return (x * jnp.exp2(power)).astype(jnp.bfloat16), jnp.broadcast_to(power, x.shape).T[0:1, :]


def restored(x, power_row):
    down = jnp.broadcast_to(jnp.exp2(-power_row), (128, 128)).T
    return (x.astype(jnp.float32) * down).astype(jnp.bfloat16)


def pack_kernel(
    where_ref, k_ref, v_ref, q_ref, ids_ref, mine_ref, mine_powers_ref, mine_q_ref, other_ref, place_ref, powers
):
    core = where_ref[2]
    own = [where_ref[0], where_ref[1], core, jnp.where(core == 0, where_ref[0], where_ref[1])]
    for i in range(4):
        place_ref[i : i + 1, :] = jnp.full((1, 128), own[i], jnp.int32)

    def cache(head, out_ref):
        def one_block(b, carry):
            at = pl.multiple_of(b * BLOCK, BLOCK)
            rows = jnp.concatenate([k_ref[head, pl.ds(at, BLOCK), :], v_ref[head, pl.ds(at, BLOCK), :]], axis=0)
            out, row = scaled(rows.astype(jnp.float32))
            out_ref[pl.ds(pl.multiple_of(b * PAIR, PAIR), PAIR), :] = out
            powers[pl.ds(b, 1), :] = row
            return carry

        lax.fori_loop(0, BLK_DEV, one_block, 0, unroll=4)
        return powers[...].astype(jnp.bfloat16)

    def queries(head, out_ref, first):
        rows = lax.broadcasted_iota(jnp.int32, (16, 128), 0)
        extra = ids_ref[head].astype(jnp.float32)
        for i in range(ROWS // 128):
            out, row = scaled(q_ref[head, i * 128 : (i + 1) * 128, :].astype(jnp.float32))
            out_ref[first + i * 128 : first + (i + 1) * 128, :] = out
            extra = jnp.where(rows == i, row, extra)
        out_ref[first + ROWS : first + QROWS, :] = extra.astype(jnp.bfloat16)

    mine_powers_ref[...] = cache(core, mine_ref)
    other_ref[SHARE : SHARE + BLK_DEV, :] = cache(1 - core, other_ref)
    queries(1 - core, mine_q_ref, 0)
    queries(core, other_ref, SHARE + BLK_DEV)


def window_kernel(first_ref, q_ref, k_ref, v_ref, o_ref):
    for rc in range(2):
        s = lax.dot_general(
            k_ref[pl.ds(128 * rc, 256), :],
            q_ref[rc],
            (((1,), (1,)), ((), ())),
            preferred_element_type=jnp.float32,
        )
        kpos = lax.broadcasted_iota(jnp.int32, s.shape, 0) - 128
        qpos = lax.broadcasted_iota(jnp.int32, s.shape, 1) & 127
        allowed = (kpos <= qpos) & (kpos > qpos - 128)
        if rc == 0:
            allowed = allowed & ((kpos >= 0) | (first_ref[0] == 0))
        s = jnp.where(allowed, s, LOWEST)
        top = jnp.max(s, axis=0, keepdims=True)
        p = jnp.exp2((s - top) * EXPO)
        total = jnp.sum(p, axis=0, keepdims=True)
        out = lax.dot_general(
            v_ref[pl.ds(128 * rc, 256), :],
            p.astype(jnp.bfloat16),
            (((0,), (0,)), ((), ())),
            preferred_element_type=jnp.float32,
        )
        o_ref[rc] = out / total


def memory_kernel(deltas, count_ref, place_ref, power_at_ref, where_ref, q_ref, powers_ref, kv_ref, *rest):
    o_refs = rest[: len(deltas)]
    q_buf, acc, top_s, sum_s = rest[len(deltas) :]
    eye = lax.broadcasted_iota(jnp.int32, (128, 128), 0) == lax.broadcasted_iota(jnp.int32, (128, 128), 1)
    low = lax.broadcasted_iota(jnp.int32, (1, 128), 1) < BLOCK

    def back(x, power_row):
        scale = jnp.where(eye, jnp.exp2(-power_row), 0.0).astype(jnp.bfloat16)
        return jnp.dot(scale, x, preferred_element_type=jnp.float32).astype(jnp.bfloat16)

    def attend(index, rc, count, step):
        keys, values = [], []
        for i in range(0, STEP, 2):
            places = [pl.multiple_of(place_ref[index, step * STEP + i + j], 16) for j in range(2)]
            rows = [powers_ref[pl.ds(power_at_ref[index, step * STEP + i + j], 1), :] for j in range(2)]
            turned = [pltpu.roll(row, BLOCK, 1) for row in rows]
            both = jnp.concatenate([kv_ref[pl.ds(at, BLOCK), :] for at in places], axis=0)
            keys.append(back(both, jnp.where(low, rows[0], turned[1])))
            both = jnp.concatenate([kv_ref[pl.ds(at + BLOCK, BLOCK), :] for at in places], axis=0)
            down = jnp.exp2(-jnp.where(low, turned[0], rows[1]))
            values.append((both.T.astype(jnp.float32) * down).astype(jnp.bfloat16))
        s = lax.dot_general(
            jnp.concatenate(keys, axis=0), q_buf[rc], (((1,), (1,)), ((), ())), preferred_element_type=jnp.float32
        )
        s = jnp.concatenate(
            [
                jnp.where(step * STEP + i < count, s[i * BLOCK : (i + 1) * BLOCK], LOWEST)
                for i in range(STEP)
            ],
            axis=0,
        )
        return s, jnp.max(s, axis=0, keepdims=True), jnp.concatenate(values, axis=1)

    for o_ref, delta in zip(o_refs, deltas):
        peer = lax.rem(where_ref[3, 0] + delta, LINE)
        counts = [count_ref[peer * 2 + rc] for rc in range(2)]
        for rc in range(2):
            index = peer * 2 + rc
            first = pl.multiple_of(index * QROWS, 16)
            extra = q_ref[pl.ds(first + ROWS, 16), :].astype(jnp.float32)
            for i in range(ROWS // 128):
                q_buf[rc, i * 128 : (i + 1) * 128, :] = back(
                    q_ref[pl.ds(first + i * 128, 128), :], extra[i : i + 1, :]
                )
            s, top, values = attend(index, rc, counts[rc], 0)
            p = jnp.exp2((s - top) * EXPO)
            top_s[rc] = top
            sum_s[rc] = jnp.sum(p, axis=0, keepdims=True)
            acc[rc] = jnp.dot(values, p.astype(jnp.bfloat16), preferred_element_type=jnp.float32)

        def one_step(step, carry):
            for rc in range(2):
                s, top, values = attend(peer * 2 + rc, rc, counts[rc], step)
                top = jnp.maximum(top_s[rc], top)
                p = jnp.exp2((s - top) * EXPO)
                alpha = jnp.exp2((top_s[rc] - top) * EXPO)
                top_s[rc] = top
                sum_s[rc] = sum_s[rc] * alpha + jnp.sum(p, axis=0, keepdims=True)
                acc[rc] = acc[rc] * alpha + jnp.dot(values, p.astype(jnp.bfloat16), preferred_element_type=jnp.float32)
            return carry

        lax.fori_loop(1, (jnp.maximum(counts[0], counts[1]) + STEP - 1) // STEP, one_step, 0)
        rows = lax.broadcasted_iota(jnp.int32, (16, ROWS), 0)
        pieces = jnp.zeros((16, ROWS), jnp.float32)
        for rc in range(2):
            some = counts[rc] > 0
            total = jnp.where(some, sum_s[rc], 1.0)
            o_ref[rc * HEAD : (rc + 1) * HEAD, :] = (acc[rc] * jnp.where(some, 1.0 / total, 0.0)).astype(jnp.bfloat16)
            level = jnp.where(some, top_s[rc] * EXPO + jnp.log2(total), LOWEST)
            high = level.astype(jnp.bfloat16).astype(jnp.float32)
            mid = (level - high).astype(jnp.bfloat16).astype(jnp.float32)
            for i, piece in enumerate((high, mid, level - high - mid)):
                pieces = jnp.where(rows == 3 * rc + i, piece, pieces)
        o_ref[2 * HEAD :, :] = pieces.astype(jnp.bfloat16)


def merge_kernel(*refs):
    part_refs = refs[:LINE]
    window_ref, gate_ref, o_ref = refs[LINE:]
    gate = gate_ref[...]
    for rc in range(2):
        levels = []
        for i in range(LINE):
            pieces = part_refs[i][2 * HEAD :, :].astype(jnp.float32)[3 * rc : 3 * rc + 3, :]
            levels.append(pieces[0:1] + pieces[1:2] + pieces[2:3])
        top = functools.reduce(jnp.maximum, levels)
        shares = [jnp.exp2(level - top) for level in levels]
        scale = gate / functools.reduce(jnp.add, shares)
        mixed = (1.0 - gate) * window_ref[rc]
        for i in range(LINE):
            mixed = mixed + part_refs[i][rc * HEAD : (rc + 1) * HEAD, :].astype(jnp.float32) * (shares[i] * scale)
        for g in range(4):
            flat = mixed[:, g * 128 : (g + 1) * 128].T.astype(jnp.bfloat16)
            for x in range(X):
                o_ref[x * 2 + rc, :, g * 128 : (g + 1) * 128] = flat[x * 32 : (x + 1) * 32, :]


def on_device(queries, keys, values, mem_keys, mem_values, mem_ids, gate_logits):
    z, y, core = lax.axis_index("z"), lax.axis_index("y"), lax.axis_index("core")
    first_core = core == 0
    smem = pl.BlockSpec(memory_space=pltpu.SMEM)
    vmem = pl.BlockSpec(memory_space=pltpu.VMEM)
    swap = [(0, 1), (1, 0)]

    def mine_and_other(array):
        return jnp.where(first_core, array[0], array[1]), jnp.where(first_core, array[1], array[0])

    def by_core(mine, other):
        return jnp.where(first_core, mine, other), jnp.where(first_core, other, mine)

    by_head = queries.reshape(128, 2, 4, HEAD).transpose(1, 2, 0, 3).reshape(2, ROWS, HEAD)
    ids = jnp.concatenate([mem_ids // 64, mem_ids % 64], axis=2).astype(jnp.bfloat16)
    ids = jnp.pad(ids, ((0, 0), (4, 11), (0, HEAD - 2 * TOPK)))
    mine, mine_powers, mine_q, other, placed = pl.pallas_call(
        pack_kernel,
        out_shape=[
            jax.ShapeDtypeStruct((SHARE, HEAD), jnp.bfloat16),
            jax.ShapeDtypeStruct((BLK_DEV, HEAD), jnp.bfloat16),
            jax.ShapeDtypeStruct((QROWS, HEAD), jnp.bfloat16),
            jax.ShapeDtypeStruct((SHARE + BLK_DEV + QROWS, HEAD), jnp.bfloat16),
            jax.ShapeDtypeStruct((8, 128), jnp.int32),
        ],
        in_specs=[smem] + [vmem] * 4,
        out_specs=[vmem] * 5,
        scratch_shapes=[pltpu.VMEM((BLK_DEV, HEAD), jnp.float32)],
        compiler_params=pltpu.CompilerParams(vmem_limit_bytes=16 << 20),
        cost_estimate=pl.CostEstimate(flops=1 << 22, bytes_accessed=3 << 20, transcendentals=1 << 13),
        name="pack",
    )(
        jnp.stack([z, y, core]).astype(jnp.int32),
        mem_keys.transpose(1, 0, 2),
        mem_values.transpose(1, 0, 2),
        by_head,
        ids,
    )
    theirs = lax.ppermute(other, "core", swap)
    their_cache, their_powers, their_q = jnp.split(theirs, [SHARE, SHARE + BLK_DEV])
    shard = jnp.concatenate(
        [mine, their_cache, mine_powers, their_powers, *by_core(mine_q, their_q)], axis=0
    ).astype(jnp.float16)
    gathered = lax.all_gather(shard, SEQ, axis_index_groups=KV_LINES, tiled=True)
    parts = gathered.reshape(LINE, SHARD, HEAD)
    lists = lax.ppermute(parts[:, SHARD - 2 * QROWS :], "core", swap)
    lists = lists.reshape(2 * LINE * QROWS, HEAD).astype(jnp.bfloat16)
    cache = gathered.astype(jnp.bfloat16)
    powers = parts[:, CACHE : CACHE + 2 * BLK_DEV].reshape(2 * LINE * BLK_DEV, HEAD).astype(jnp.float32)

    coded = lists.reshape(2 * LINE, QROWS, HEAD)[:, ROWS + 4, : 2 * TOPK].astype(jnp.int32)
    wanted = coded[:, :TOPK] * 64 + coded[:, TOPK:]
    owner, local = wanted // BLK_DEV, wanted % BLK_DEV
    owner_z, owner_y, owner_core = owner // (2 * Y), (owner // 2) % Y, owner % 2
    my_z, my_y, my_core = (placed[i : i + 1, :TOPK] for i in range(3))
    here = jnp.where(my_core == 0, owner_z == my_z, owner_y == my_y)
    position = jnp.where(my_core == 0, owner_y, owner_z)
    index = (position * 2 + (owner_core != my_core).astype(jnp.int32)) * BLK_DEV + local
    rank = jnp.sum(
        (here[:, None, :] & (jnp.arange(TOPK)[None, None, :] < jnp.arange(TOPK)[None, :, None])).astype(jnp.int32),
        axis=2,
    )
    match = here[:, :, None] & (rank[:, :, None] == jnp.arange(BLK_DEV)[None, None, :])
    indices = jnp.sum(jnp.where(match, index[:, :, None], 0), axis=1)
    places = (indices // (2 * BLK_DEV)) * SHARD + (indices % (2 * BLK_DEV)) * PAIR
    counts = jnp.sum(here.astype(jnp.int32), axis=1)

    returned = {}
    for deltas in WAVES:
        partials = pl.pallas_call(
            functools.partial(memory_kernel, deltas),
            out_shape=[jax.ShapeDtypeStruct((OROWS, ROWS), jnp.bfloat16)] * len(deltas),
            in_specs=[smem] * 4 + [vmem] * 3,
            out_specs=[vmem] * len(deltas),
            scratch_shapes=[
                pltpu.VMEM((2, ROWS, HEAD), jnp.bfloat16),
                pltpu.VMEM((2, HEAD, ROWS), jnp.float32),
                pltpu.VMEM((2, 1, ROWS), jnp.float32),
                pltpu.VMEM((2, 1, ROWS), jnp.float32),
            ],
            compiler_params=pltpu.CompilerParams(vmem_limit_bytes=24 << 20),
            cost_estimate=pl.CostEstimate(
                flops=len(deltas) * 16 * ROWS * BLOCK * HEAD * 8,
                bytes_accessed=len(deltas) << 20,
                transcendentals=len(deltas) * 16 * ROWS * BLOCK,
            ),
            name="memory",
        )(counts, places, indices, placed, lists, powers, cache)
        for delta, partial in zip(deltas, partials):
            returned[delta] = shift(partial, Q_LINES, delta) if delta else partial

    q_mine, q_other = mine_and_other(by_head)
    k_mine, k_other = mine_and_other(keys.transpose(1, 0, 2))
    v_mine, v_other = mine_and_other(values.transpose(1, 0, 2))
    near = lax.ppermute(jnp.concatenate([q_other, k_other, v_other], axis=0), "core", swap)
    q_first, q_second = by_core(q_mine, near[:ROWS])
    k_first, k_second = by_core(k_mine, near[ROWS : ROWS + 128])
    v_first, v_second = by_core(v_mine, near[ROWS + 128 :])
    onward = [(2 * i + c, 2 * i + 2 + c) for i in range(Z * Y - 1) for c in range(2)]
    before = lax.ppermute(jnp.concatenate([k_second, v_second], axis=0), SEQ, onward)
    is_first = ((z == 0) & (y == 0)).astype(jnp.int32).reshape(1)
    window = pl.pallas_call(
        window_kernel,
        out_shape=jax.ShapeDtypeStruct((2, HEAD, ROWS), jnp.float32),
        in_specs=[smem] + [vmem] * 3,
        out_specs=vmem,
        compiler_params=pltpu.CompilerParams(vmem_limit_bytes=16 << 20),
        cost_estimate=pl.CostEstimate(
            flops=4 * 2 * ROWS * 256 * HEAD, bytes_accessed=1 << 20, transcendentals=2 * ROWS * 256
        ),
        name="window",
    )(
        is_first,
        jnp.stack([q_first, q_second]),
        jnp.concatenate([before[:128], k_first, k_second], axis=0),
        jnp.concatenate([before[128:], v_first, v_second], axis=0),
    )

    gate = jax.nn.sigmoid(gate_logits).reshape(2, 4)
    gate = jnp.repeat(jnp.where(first_core, gate[0], gate[1]), 128)[None, :]
    mixed = pl.pallas_call(
        merge_kernel,
        out_shape=jax.ShapeDtypeStruct((2 * X, 32, ROWS), jnp.bfloat16),
        in_specs=[vmem] * (LINE + 2),
        out_specs=vmem,
        compiler_params=pltpu.CompilerParams(vmem_limit_bytes=16 << 20),
        cost_estimate=pl.CostEstimate(flops=1 << 22, bytes_accessed=4 << 20, transcendentals=1 << 13),
        name="merge",
    )(*[returned[d] for d in range(LINE)], window, gate)
    rows = lax.all_to_all(mixed, ("head", "core"), split_axis=0, concat_axis=0, tiled=True)
    return rows.transpose(1, 0, 2).reshape(32, 2 * X * ROWS)


def solution(mesh):
    fine = Mesh(mesh.devices.reshape(Z, Y, 2, X), ("z", "y", "core", "head"))
    placed = (
        P(SEQ, "head", None),
        P(SEQ, "head", None),
        P(SEQ, "head", None),
        P(SEQ, "head", None),
        P(SEQ, "head", None),
        P("head", SEQ, None),
        P("head"),
    )
    return jax.shard_map(
        on_device, mesh=fine, in_specs=placed, out_specs=P(SEQ + ("head",), None), check_vma=False
    )
```

```python
import functools
import math

import jax
import jax.numpy as jnp
from jax import lax
from jax.experimental import pallas as pl
from jax.experimental.pallas import tpu as pltpu
from jax.sharding import Mesh
from jax.sharding import PartitionSpec as P

Z, Y, X = 8, 8, 4
LINE = 8
BLOCK = 64
TOPK = 32
BLK_DEV = 16
HEAD = 128
ROWS = 512
QROWS = ROWS + 16
PAIR = 2 * BLOCK
SHARE = BLK_DEV * PAIR
CACHE = 2 * SHARE
SHARD = CACHE + 2 * BLK_DEV + 2 * QROWS
OROWS = 2 * HEAD + 16
STEP = 8
LOWEST = -3.0e38
EXPO = HEAD**-0.5 * math.log2(math.e)
SEQ = ("z", "y", "core")


def seq_index(z, y, core):
    return (z * Y + y) * 2 + core


Y_LINES = [[[seq_index(z, y, core) for y in range(Y)] for z in range(Z)] for core in range(2)]
Z_LINES = [[[seq_index(z, y, core) for z in range(Z)] for y in range(Y)] for core in range(2)]
KV_LINES = Y_LINES[0] + Z_LINES[1]
Q_LINES = Z_LINES[0] + Y_LINES[1]


def scaled(x):
    largest = jnp.max(jnp.abs(x), axis=1, keepdims=True)
    power = 14.0 - jnp.floor(jnp.log2(jnp.maximum(largest, 1e-37)))
    power = jnp.clip(power, -113.0, 126.0)
    return (x * jnp.exp2(power)).astype(jnp.bfloat16), jnp.broadcast_to(power, x.shape).T[0:1, :]


def restored(x, power_row):
    down = jnp.broadcast_to(jnp.exp2(-power_row), (128, 128)).T
    return (x.astype(jnp.float32) * down).astype(jnp.bfloat16)


def pack_kernel(
    where_ref, k_ref, v_ref, q_ref, ids_ref, mine_ref, mine_powers_ref, mine_q_ref, other_ref, place_ref, powers
):
    for i in range(3):
        place_ref[i : i + 1, :] = jnp.full((1, 128), where_ref[i], jnp.int32)
    core = where_ref[2]

    def cache(head, out_ref):
        def one_block(b, carry):
            at = pl.multiple_of(b * BLOCK, BLOCK)
            rows = jnp.concatenate([k_ref[head, pl.ds(at, BLOCK), :], v_ref[head, pl.ds(at, BLOCK), :]], axis=0)
            out, row = scaled(rows.astype(jnp.float32))
            out_ref[pl.ds(pl.multiple_of(b * PAIR, PAIR), PAIR), :] = out
            powers[pl.ds(b, 1), :] = row
            return carry

        lax.fori_loop(0, BLK_DEV, one_block, 0, unroll=4)
        return powers[...].astype(jnp.bfloat16)

    def queries(head, out_ref, first):
        rows = lax.broadcasted_iota(jnp.int32, (16, 128), 0)
        extra = ids_ref[head].astype(jnp.float32)
        for i in range(ROWS // 128):
            out, row = scaled(q_ref[head, i * 128 : (i + 1) * 128, :].astype(jnp.float32))
            out_ref[first + i * 128 : first + (i + 1) * 128, :] = out
            extra = jnp.where(rows == i, row, extra)
        out_ref[first + ROWS : first + QROWS, :] = extra.astype(jnp.bfloat16)

    mine_powers_ref[...] = cache(core, mine_ref)
    other_ref[SHARE : SHARE + BLK_DEV, :] = cache(1 - core, other_ref)
    queries(1 - core, mine_q_ref, 0)
    queries(core, other_ref, SHARE + BLK_DEV)


def window_kernel(first_ref, q_ref, k_ref, v_ref, o_ref):
    for rc in range(2):
        s = lax.dot_general(
            k_ref[pl.ds(128 * rc, 256), :],
            q_ref[rc],
            (((1,), (1,)), ((), ())),
            preferred_element_type=jnp.float32,
        )
        kpos = lax.broadcasted_iota(jnp.int32, s.shape, 0) - 128
        qpos = lax.broadcasted_iota(jnp.int32, s.shape, 1) & 127
        allowed = (kpos <= qpos) & (kpos > qpos - 128)
        if rc == 0:
            allowed = allowed & ((kpos >= 0) | (first_ref[0] == 0))
        s = jnp.where(allowed, s, LOWEST)
        top = jnp.max(s, axis=0, keepdims=True)
        p = jnp.exp2((s - top) * EXPO)
        total = jnp.sum(p, axis=0, keepdims=True)
        out = lax.dot_general(
            v_ref[pl.ds(128 * rc, 256), :],
            p.astype(jnp.bfloat16),
            (((0,), (0,)), ((), ())),
            preferred_element_type=jnp.float32,
        )
        o_ref[rc] = out / total


def memory_kernel(count_ref, place_ref, power_at_ref, q_ref, powers_ref, kv_ref, o_ref, stage, q_buf, acc, top_s, sum_s, out_sems):
    eye = lax.broadcasted_iota(jnp.int32, (128, 128), 0) == lax.broadcasted_iota(jnp.int32, (128, 128), 1)
    low = lax.broadcasted_iota(jnp.int32, (1, 128), 1) < BLOCK

    def back(x, power_row):
        scale = jnp.where(eye, jnp.exp2(-power_row), 0.0).astype(jnp.bfloat16)
        return jnp.dot(scale, x, preferred_element_type=jnp.float32).astype(jnp.bfloat16)

    def send(peer):
        return pltpu.make_async_copy(stage.at[peer % 2], o_ref.at[peer], out_sems.at[peer % 2])

    def attend(index, rc, count, step):
        keys, values = [], []
        for i in range(0, STEP, 2):
            places = [pl.multiple_of(place_ref[index, step * STEP + i + j], 16) for j in range(2)]
            rows = [powers_ref[pl.ds(power_at_ref[index, step * STEP + i + j], 1), :] for j in range(2)]
            turned = [pltpu.roll(row, BLOCK, 1) for row in rows]
            both = jnp.concatenate([kv_ref[pl.ds(at, BLOCK), :] for at in places], axis=0)
            keys.append(back(both, jnp.where(low, rows[0], turned[1])))
            both = jnp.concatenate([kv_ref[pl.ds(at + BLOCK, BLOCK), :] for at in places], axis=0)
            down = jnp.exp2(-jnp.where(low, turned[0], rows[1]))
            values.append((both.T.astype(jnp.float32) * down).astype(jnp.bfloat16))
        s = lax.dot_general(
            jnp.concatenate(keys, axis=0), q_buf[rc], (((1,), (1,)), ((), ())), preferred_element_type=jnp.float32
        )
        s = jnp.concatenate(
            [
                jnp.where(step * STEP + i < count, s[i * BLOCK : (i + 1) * BLOCK], LOWEST)
                for i in range(STEP)
            ],
            axis=0,
        )
        top = jnp.max(s, axis=0, keepdims=True)
        return s, top, jnp.concatenate(values, axis=1)

    for peer in range(LINE):
        slot = peer % 2
        counts = [count_ref[peer * 2 + rc] for rc in range(2)]
        for rc in range(2):
            index = peer * 2 + rc
            first = index * QROWS
            extra = q_ref[first + ROWS : first + QROWS, :].astype(jnp.float32)
            for i in range(ROWS // 128):
                q_buf[rc, i * 128 : (i + 1) * 128, :] = back(
                    q_ref[first + i * 128 : first + (i + 1) * 128, :], extra[i : i + 1, :]
                )
            s, top, values = attend(index, rc, counts[rc], 0)
            p = jnp.exp2((s - top) * EXPO)
            top_s[rc] = top
            sum_s[rc] = jnp.sum(p, axis=0, keepdims=True)
            acc[rc] = jnp.dot(values, p.astype(jnp.bfloat16), preferred_element_type=jnp.float32)

        def one_step(step, carry):
            for rc in range(2):
                s, top, values = attend(peer * 2 + rc, rc, counts[rc], step)
                top = jnp.maximum(top_s[rc], top)
                p = jnp.exp2((s - top) * EXPO)
                alpha = jnp.exp2((top_s[rc] - top) * EXPO)
                top_s[rc] = top
                sum_s[rc] = sum_s[rc] * alpha + jnp.sum(p, axis=0, keepdims=True)
                acc[rc] = acc[rc] * alpha + jnp.dot(values, p.astype(jnp.bfloat16), preferred_element_type=jnp.float32)
            return carry

        lax.fori_loop(1, (jnp.maximum(counts[0], counts[1]) + STEP - 1) // STEP, one_step, 0)
        if peer >= 2:
            send(peer - 2).wait()
        rows = lax.broadcasted_iota(jnp.int32, (16, ROWS), 0)
        pieces = jnp.zeros((16, ROWS), jnp.float32)
        for rc in range(2):
            some = counts[rc] > 0
            total = jnp.where(some, sum_s[rc], 1.0)
            stage[slot, rc * HEAD : (rc + 1) * HEAD, :] = (acc[rc] * jnp.where(some, 1.0 / total, 0.0)).astype(jnp.bfloat16)
            level = jnp.where(some, top_s[rc] * EXPO + jnp.log2(total), LOWEST)
            high = level.astype(jnp.bfloat16).astype(jnp.float32)
            mid = (level - high).astype(jnp.bfloat16).astype(jnp.float32)
            for i, piece in enumerate((high, mid, level - high - mid)):
                pieces = jnp.where(rows == 3 * rc + i, piece, pieces)
        stage[slot, 2 * HEAD :, :] = pieces.astype(jnp.bfloat16)
        send(peer).start()
    send(LINE - 2).wait()
    send(LINE - 1).wait()


def merge_kernel(part_ref, window_ref, gate_ref, o_ref):
    gate = gate_ref[...]
    for rc in range(2):
        levels = []
        for i in range(LINE):
            pieces = part_ref[i, 2 * HEAD :, :].astype(jnp.float32)[3 * rc : 3 * rc + 3, :]
            levels.append(pieces[0:1] + pieces[1:2] + pieces[2:3])
        top = functools.reduce(jnp.maximum, levels)
        shares = [jnp.exp2(level - top) for level in levels]
        scale = gate / functools.reduce(jnp.add, shares)
        mixed = (1.0 - gate) * window_ref[rc]
        for i in range(LINE):
            mixed = mixed + part_ref[i, rc * HEAD : (rc + 1) * HEAD, :].astype(jnp.float32) * (shares[i] * scale)
        for g in range(4):
            flat = mixed[:, g * 128 : (g + 1) * 128].T.astype(jnp.bfloat16)
            for x in range(X):
                o_ref[x * 2 + rc, :, g * 128 : (g + 1) * 128] = flat[x * 32 : (x + 1) * 32, :]


def on_device(queries, keys, values, mem_keys, mem_values, mem_ids, gate_logits):
    z, y, core = lax.axis_index("z"), lax.axis_index("y"), lax.axis_index("core")
    first_core = core == 0
    smem = pl.BlockSpec(memory_space=pltpu.SMEM)
    vmem = pl.BlockSpec(memory_space=pltpu.VMEM)
    swap = [(0, 1), (1, 0)]

    def mine_and_other(array):
        return jnp.where(first_core, array[0], array[1]), jnp.where(first_core, array[1], array[0])

    def by_core(mine, other):
        return jnp.where(first_core, mine, other), jnp.where(first_core, other, mine)

    by_head = queries.reshape(128, 2, 4, HEAD).transpose(1, 2, 0, 3).reshape(2, ROWS, HEAD)
    ids = jnp.concatenate([mem_ids // 64, mem_ids % 64], axis=2).astype(jnp.bfloat16)
    ids = jnp.pad(ids, ((0, 0), (4, 11), (0, HEAD - 2 * TOPK)))
    mine, mine_powers, mine_q, other, placed = pl.pallas_call(
        pack_kernel,
        out_shape=[
            jax.ShapeDtypeStruct((SHARE, HEAD), jnp.bfloat16),
            jax.ShapeDtypeStruct((BLK_DEV, HEAD), jnp.bfloat16),
            jax.ShapeDtypeStruct((QROWS, HEAD), jnp.bfloat16),
            jax.ShapeDtypeStruct((SHARE + BLK_DEV + QROWS, HEAD), jnp.bfloat16),
            jax.ShapeDtypeStruct((8, 128), jnp.int32),
        ],
        in_specs=[smem] + [vmem] * 4,
        out_specs=[vmem] * 5,
        scratch_shapes=[pltpu.VMEM((BLK_DEV, HEAD), jnp.float32)],
        compiler_params=pltpu.CompilerParams(vmem_limit_bytes=16 << 20),
        cost_estimate=pl.CostEstimate(flops=1 << 22, bytes_accessed=3 << 20, transcendentals=1 << 13),
        name="pack",
    )(
        jnp.stack([z, y, core]).astype(jnp.int32),
        mem_keys.transpose(1, 0, 2),
        mem_values.transpose(1, 0, 2),
        by_head,
        ids,
    )
    theirs = lax.ppermute(other, "core", swap)
    their_cache, their_powers, their_q = jnp.split(theirs, [SHARE, SHARE + BLK_DEV])
    shard = jnp.concatenate(
        [mine, their_cache, mine_powers, their_powers, *by_core(mine_q, their_q)], axis=0
    ).astype(jnp.float16)
    gathered = lax.all_gather(shard, SEQ, axis_index_groups=KV_LINES, tiled=True)
    parts = gathered.reshape(LINE, SHARD, HEAD)
    lists = lax.ppermute(parts[:, SHARD - 2 * QROWS :], "core", swap)
    lists = lists.reshape(2 * LINE * QROWS, HEAD).astype(jnp.bfloat16)
    cache = gathered.astype(jnp.bfloat16)
    powers = parts[:, CACHE : CACHE + 2 * BLK_DEV].reshape(2 * LINE * BLK_DEV, HEAD).astype(jnp.float32)

    coded = lists.reshape(2 * LINE, QROWS, HEAD)[:, ROWS + 4, : 2 * TOPK].astype(jnp.int32)
    wanted = coded[:, :TOPK] * 64 + coded[:, TOPK:]
    owner, local = wanted // BLK_DEV, wanted % BLK_DEV
    owner_z, owner_y, owner_core = owner // (2 * Y), (owner // 2) % Y, owner % 2
    my_z, my_y, my_core = (placed[i : i + 1, :TOPK] for i in range(3))
    here = jnp.where(my_core == 0, owner_z == my_z, owner_y == my_y)
    position = jnp.where(my_core == 0, owner_y, owner_z)
    index = (position * 2 + (owner_core != my_core).astype(jnp.int32)) * BLK_DEV + local
    rank = jnp.sum(
        (here[:, None, :] & (jnp.arange(TOPK)[None, None, :] < jnp.arange(TOPK)[None, :, None])).astype(jnp.int32),
        axis=2,
    )
    match = here[:, :, None] & (rank[:, :, None] == jnp.arange(BLK_DEV)[None, None, :])
    indices = jnp.sum(jnp.where(match, index[:, :, None], 0), axis=1)
    places = (indices // (2 * BLK_DEV)) * SHARD + (indices % (2 * BLK_DEV)) * PAIR
    counts = jnp.sum(here.astype(jnp.int32), axis=1)

    partial = pl.pallas_call(
        memory_kernel,
        out_shape=pltpu.HBM((LINE, OROWS, ROWS), jnp.bfloat16),
        in_specs=[smem] * 3 + [vmem] * 3,
        out_specs=pl.BlockSpec(memory_space=pltpu.HBM),
        scratch_shapes=[
            pltpu.VMEM((2, OROWS, ROWS), jnp.bfloat16),
            pltpu.VMEM((2, ROWS, HEAD), jnp.bfloat16),
            pltpu.VMEM((2, HEAD, ROWS), jnp.float32),
            pltpu.VMEM((2, 1, ROWS), jnp.float32),
            pltpu.VMEM((2, 1, ROWS), jnp.float32),
            pltpu.SemaphoreType.DMA((2,)),
        ],
        compiler_params=pltpu.CompilerParams(vmem_limit_bytes=24 << 20),
        cost_estimate=pl.CostEstimate(
            flops=4 * 64 * ROWS * BLOCK * HEAD, bytes_accessed=6 << 20, transcendentals=64 * ROWS * BLOCK
        ),
        name="memory",
    )(counts, places, indices, lists, powers, cache)
    returned = lax.all_to_all(
        partial, SEQ, split_axis=0, concat_axis=0, axis_index_groups=Q_LINES, tiled=True
    )

    q_mine, q_other = mine_and_other(by_head)
    k_mine, k_other = mine_and_other(keys.transpose(1, 0, 2))
    v_mine, v_other = mine_and_other(values.transpose(1, 0, 2))
    near = lax.ppermute(jnp.concatenate([q_other, k_other, v_other], axis=0), "core", swap)
    q_first, q_second = by_core(q_mine, near[:ROWS])
    k_first, k_second = by_core(k_mine, near[ROWS : ROWS + 128])
    v_first, v_second = by_core(v_mine, near[ROWS + 128 :])
    onward = [(2 * i + c, 2 * i + 2 + c) for i in range(Z * Y - 1) for c in range(2)]
    before = lax.ppermute(jnp.concatenate([k_second, v_second], axis=0), SEQ, onward)
    is_first = ((z == 0) & (y == 0)).astype(jnp.int32).reshape(1)
    window = pl.pallas_call(
        window_kernel,
        out_shape=jax.ShapeDtypeStruct((2, HEAD, ROWS), jnp.float32),
        in_specs=[smem] + [vmem] * 3,
        out_specs=vmem,
        compiler_params=pltpu.CompilerParams(vmem_limit_bytes=16 << 20),
        cost_estimate=pl.CostEstimate(
            flops=4 * 2 * ROWS * 256 * HEAD, bytes_accessed=1 << 20, transcendentals=2 * ROWS * 256
        ),
        name="window",
    )(
        is_first,
        jnp.stack([q_first, q_second]),
        jnp.concatenate([before[:128], k_first, k_second], axis=0),
        jnp.concatenate([before[128:], v_first, v_second], axis=0),
    )

    gate = jax.nn.sigmoid(gate_logits).reshape(2, 4)
    gate = jnp.repeat(jnp.where(first_core, gate[0], gate[1]), 128)[None, :]
    mixed = pl.pallas_call(
        merge_kernel,
        out_shape=jax.ShapeDtypeStruct((2 * X, 32, ROWS), jnp.bfloat16),
        in_specs=[vmem] * 3,
        out_specs=vmem,
        compiler_params=pltpu.CompilerParams(vmem_limit_bytes=16 << 20),
        cost_estimate=pl.CostEstimate(flops=1 << 22, bytes_accessed=4 << 20, transcendentals=1 << 13),
        name="merge",
    )(returned, window, gate)
    rows = lax.all_to_all(mixed, ("head", "core"), split_axis=0, concat_axis=0, tiled=True)
    return rows.transpose(1, 0, 2).reshape(32, 2 * X * ROWS)


def solution(mesh):
    fine = Mesh(mesh.devices.reshape(Z, Y, 2, X), ("z", "y", "core", "head"))
    placed = (
        P(SEQ, "head", None),
        P(SEQ, "head", None),
        P(SEQ, "head", None),
        P(SEQ, "head", None),
        P(SEQ, "head", None),
        P("head", SEQ, None),
        P("head"),
    )
    return jax.shard_map(
        on_device, mesh=fine, in_specs=placed, out_specs=P(SEQ + ("head",), None), check_vma=False
    )
```

```python
import functools
import math

import jax
import jax.numpy as jnp
from jax import lax
from jax.experimental import pallas as pl
from jax.experimental.pallas import tpu as pltpu
from jax.sharding import Mesh
from jax.sharding import PartitionSpec as P

Z, Y, X = 8, 8, 4
LINE = 8
BLOCK = 64
TOPK = 32
BLK_DEV = 16
HEAD = 128
ROWS = 512
QROWS = ROWS + 16
PAIR = 2 * BLOCK
SHARE = BLK_DEV * PAIR
CACHE = 2 * SHARE
SHARD = CACHE + 2 * BLK_DEV + 2 * QROWS
OROWS = 2 * HEAD + 16
STEP = 8
LOWEST = -3.0e38
EXPO = HEAD**-0.5 * math.log2(math.e)
SEQ = ("z", "y", "core")


def seq_index(z, y, core):
    return (z * Y + y) * 2 + core


Y_LINES = [[[seq_index(z, y, core) for y in range(Y)] for z in range(Z)] for core in range(2)]
Z_LINES = [[[seq_index(z, y, core) for z in range(Z)] for y in range(Y)] for core in range(2)]
KV_LINES = Y_LINES[0] + Z_LINES[1]
Q_LINES = Z_LINES[0] + Y_LINES[1]


def scaled(x):
    largest = jnp.max(jnp.abs(x), axis=1, keepdims=True)
    power = 14.0 - jnp.floor(jnp.log2(jnp.maximum(largest, 1e-37)))
    power = jnp.clip(power, -113.0, 126.0)
    return (x * jnp.exp2(power)).astype(jnp.bfloat16), jnp.broadcast_to(power, x.shape).T[0:1, :]


def restored(x, power_row):
    down = jnp.broadcast_to(jnp.exp2(-power_row), (128, 128)).T
    return (x.astype(jnp.float32) * down).astype(jnp.bfloat16)


def pack_kernel(
    where_ref, k_ref, v_ref, q_ref, ids_ref, mine_ref, mine_powers_ref, mine_q_ref, other_ref, place_ref, powers
):
    for i in range(3):
        place_ref[i : i + 1, :] = jnp.full((1, 128), where_ref[i], jnp.int32)
    core = where_ref[2]

    def cache(head, out_ref):
        def one_block(b, carry):
            at = pl.multiple_of(b * BLOCK, BLOCK)
            rows = jnp.concatenate([k_ref[head, pl.ds(at, BLOCK), :], v_ref[head, pl.ds(at, BLOCK), :]], axis=0)
            out, row = scaled(rows.astype(jnp.float32))
            out_ref[pl.ds(pl.multiple_of(b * PAIR, PAIR), PAIR), :] = out
            powers[pl.ds(b, 1), :] = row
            return carry

        lax.fori_loop(0, BLK_DEV, one_block, 0, unroll=4)
        return powers[...].astype(jnp.bfloat16)

    def queries(head, out_ref, first):
        rows = lax.broadcasted_iota(jnp.int32, (16, 128), 0)
        ids = ids_ref[head]
        coded = jnp.concatenate([ids >> 6, ids & 63, jnp.zeros((1, HEAD - 2 * TOPK), jnp.int32)], axis=1)
        extra = jnp.where(rows == ROWS // 128, coded.astype(jnp.float32), 0.0)
        for i in range(ROWS // 128):
            out, row = scaled(q_ref[head, i * 128 : (i + 1) * 128, :].astype(jnp.float32))
            out_ref[first + i * 128 : first + (i + 1) * 128, :] = out
            extra = jnp.where(rows == i, row, extra)
        out_ref[first + ROWS : first + QROWS, :] = extra.astype(jnp.bfloat16)

    mine_powers_ref[...] = cache(core, mine_ref)
    other_ref[SHARE : SHARE + BLK_DEV, :] = cache(1 - core, other_ref)
    queries(1 - core, mine_q_ref, 0)
    queries(core, other_ref, SHARE + BLK_DEV)


def window_kernel(where_ref, q_ref, k_ref, v_ref, o_ref):
    has_before = where_ref[0] + where_ref[1] + where_ref[2] > 0
    for head in range(2):
        s = lax.dot_general(
            k_ref[head], q_ref[head], (((1,), (1,)), ((), ())), preferred_element_type=jnp.float32
        )
        kpos = lax.broadcasted_iota(jnp.int32, s.shape, 0) - 128
        qpos = lax.broadcasted_iota(jnp.int32, s.shape, 1) & 127
        allowed = (kpos <= qpos) & (kpos > qpos - 128) & ((kpos >= 0) | has_before)
        s = jnp.where(allowed, s, LOWEST)
        top = jnp.max(s, axis=0, keepdims=True)
        p = jnp.exp2((s - top) * EXPO)
        total = jnp.sum(p, axis=0, keepdims=True)
        out = lax.dot_general(
            v_ref[head], p.astype(jnp.bfloat16), (((0,), (0,)), ((), ())), preferred_element_type=jnp.float32
        )
        o_ref[head ^ where_ref[2]] = out / total


def memory_kernel(count_ref, place_ref, power_at_ref, q_ref, powers_ref, kv_ref, near_ref, o_ref, stage, q_buf, acc, top_s, sum_s, out_sems):
    eye = lax.broadcasted_iota(jnp.int32, (128, 128), 0) == lax.broadcasted_iota(jnp.int32, (128, 128), 1)
    low = lax.broadcasted_iota(jnp.int32, (1, 128), 1) < BLOCK

    def back(x, power_row):
        scale = jnp.where(eye, jnp.exp2(-power_row), 0.0).astype(jnp.bfloat16)
        return jnp.dot(scale, x, preferred_element_type=jnp.float32).astype(jnp.bfloat16)

    def send(peer):
        return pltpu.make_async_copy(stage.at[peer % 2], o_ref.at[peer], out_sems.at[peer % 2])

    def attend(index, rc, count, step):
        keys, values = [], []
        for i in range(0, STEP, 2):
            places = [pl.multiple_of(place_ref[index, step * STEP + i + j], 16) for j in range(2)]
            rows = [powers_ref[pl.ds(power_at_ref[index, step * STEP + i + j], 1), :] for j in range(2)]
            turned = [pltpu.roll(row, BLOCK, 1) for row in rows]
            both = jnp.concatenate([kv_ref[pl.ds(at, BLOCK), :] for at in places], axis=0)
            keys.append(back(both, jnp.where(low, rows[0], turned[1])))
            both = jnp.concatenate([kv_ref[pl.ds(at + BLOCK, BLOCK), :] for at in places], axis=0)
            down = jnp.exp2(-jnp.where(low, turned[0], rows[1]))
            values.append((both.T.astype(jnp.float32) * down).astype(jnp.bfloat16))
        s = lax.dot_general(
            jnp.concatenate(keys, axis=0), q_buf[rc], (((1,), (1,)), ((), ())), preferred_element_type=jnp.float32
        )
        s = jnp.concatenate(
            [
                jnp.where(step * STEP + i < count, s[i * BLOCK : (i + 1) * BLOCK], LOWEST)
                for i in range(STEP)
            ],
            axis=0,
        )
        top = jnp.max(s, axis=0, keepdims=True)
        return s, top, jnp.concatenate(values, axis=1)

    for peer in range(LINE):
        slot = peer % 2
        counts = [count_ref[peer * 2 + rc] for rc in range(2)]
        for rc in range(2):
            index = peer * 2 + rc
            first = index * QROWS
            extra = q_ref[first + ROWS : first + QROWS, :].astype(jnp.float32)
            for i in range(ROWS // 128):
                q_buf[rc, i * 128 : (i + 1) * 128, :] = back(
                    q_ref[first + i * 128 : first + (i + 1) * 128, :], extra[i : i + 1, :]
                )
        held = [attend(peer * 2 + rc, rc, counts[rc], 0) for rc in range(2)]
        for rc in range(2):
            s, top, values = held[rc]
            p = jnp.exp2((s - top) * EXPO)
            top_s[rc] = top
            sum_s[rc] = jnp.sum(p, axis=0, keepdims=True)
            acc[rc] = jnp.dot(values, p.astype(jnp.bfloat16), preferred_element_type=jnp.float32)

        def one_step(step, carry):
            for rc in range(2):
                s, top, values = attend(peer * 2 + rc, rc, counts[rc], step)
                top = jnp.maximum(top_s[rc], top)
                p = jnp.exp2((s - top) * EXPO)
                alpha = jnp.exp2((top_s[rc] - top) * EXPO)
                top_s[rc] = top
                sum_s[rc] = sum_s[rc] * alpha + jnp.sum(p, axis=0, keepdims=True)
                acc[rc] = acc[rc] * alpha + jnp.dot(values, p.astype(jnp.bfloat16), preferred_element_type=jnp.float32)
            return carry

        lax.fori_loop(1, (jnp.maximum(counts[0], counts[1]) + STEP - 1) // STEP, one_step, 0)
        if peer >= 2:
            send(peer - 2).wait()
        rows = lax.broadcasted_iota(jnp.int32, (16, ROWS), 0)
        pieces = jnp.zeros((16, ROWS), jnp.float32)
        for rc in range(2):
            some = counts[rc] > 0
            total = jnp.where(some, sum_s[rc], 1.0)
            stage[slot, rc * HEAD : (rc + 1) * HEAD, :] = (acc[rc] * jnp.where(some, 1.0 / total, 0.0)).astype(jnp.bfloat16)
            level = jnp.where(some, top_s[rc] * EXPO + jnp.log2(total), LOWEST)
            high = level.astype(jnp.bfloat16).astype(jnp.float32)
            mid = (level - high).astype(jnp.bfloat16).astype(jnp.float32)
            for i, piece in enumerate((high, mid, level - high - mid)):
                pieces = jnp.where(rows == 3 * rc + i, piece, pieces)
        stage[slot, 2 * HEAD :, :] = pieces.astype(jnp.bfloat16)
        send(peer).start()
    send(LINE - 2).wait()
    send(LINE - 1).wait()


def merge_kernel(where_ref, part_ref, window_ref, their_window_ref, gate_ref, o_ref):
    gate = gate_ref[...]
    for rc in range(2):
        levels = []
        for i in range(LINE):
            pieces = part_ref[i, 2 * HEAD :, :].astype(jnp.float32)[3 * rc : 3 * rc + 3, :]
            levels.append(pieces[0:1] + pieces[1:2] + pieces[2:3])
        top = functools.reduce(jnp.maximum, levels)
        shares = [jnp.exp2(level - top) for level in levels]
        scale = gate / functools.reduce(jnp.add, shares)
        mixed = (1.0 - gate) * jnp.where(where_ref[2] == rc, window_ref[0], their_window_ref[...])
        for i in range(LINE):
            mixed = mixed + part_ref[i, rc * HEAD : (rc + 1) * HEAD, :].astype(jnp.float32) * (shares[i] * scale)
        for g in range(4):
            flat = mixed[:, g * 128 : (g + 1) * 128].T.astype(jnp.bfloat16)
            for x in range(X):
                o_ref[x * 2 + rc, :, g * 128 : (g + 1) * 128] = flat[x * 32 : (x + 1) * 32, :]


def on_device(queries, keys, values, mem_keys, mem_values, mem_ids, gate_logits):
    z, y, core = lax.axis_index("z"), lax.axis_index("y"), lax.axis_index("core")
    first_core = core == 0
    smem = pl.BlockSpec(memory_space=pltpu.SMEM)
    vmem = pl.BlockSpec(memory_space=pltpu.VMEM)
    swap = [(0, 1), (1, 0)]

    def by_core(mine, other):
        return jnp.where(first_core, mine, other), jnp.where(first_core, other, mine)

    where = jnp.stack([z, y, core]).astype(jnp.int32)
    by_head = queries.reshape(128, 2, 4, HEAD).transpose(1, 2, 0, 3).reshape(2, ROWS, HEAD)
    mine, mine_powers, mine_q, other, placed = pl.pallas_call(
        pack_kernel,
        out_shape=[
            jax.ShapeDtypeStruct((SHARE, HEAD), jnp.bfloat16),
            jax.ShapeDtypeStruct((BLK_DEV, HEAD), jnp.bfloat16),
            jax.ShapeDtypeStruct((QROWS, HEAD), jnp.bfloat16),
            jax.ShapeDtypeStruct((SHARE + BLK_DEV + QROWS, HEAD), jnp.bfloat16),
            jax.ShapeDtypeStruct((8, 128), jnp.int32),
        ],
        in_specs=[smem] + [vmem] * 4,
        out_specs=[vmem] * 5,
        scratch_shapes=[pltpu.VMEM((BLK_DEV, HEAD), jnp.float32)],
        compiler_params=pltpu.CompilerParams(vmem_limit_bytes=16 << 20),
        cost_estimate=pl.CostEstimate(flops=1 << 22, bytes_accessed=3 << 20, transcendentals=1 << 13),
        name="pack",
    )(
        where,
        mem_keys.transpose(1, 0, 2),
        mem_values.transpose(1, 0, 2),
        by_head,
        mem_ids,
    )
    near = lax.ppermute(
        jnp.concatenate([keys, values], axis=0).transpose(1, 0, 2), SEQ, [(i, i + 1) for i in range(2 * Z * Y - 1)]
    )
    theirs = lax.ppermute(other, "core", swap)
    their_cache, their_powers, their_q = jnp.split(theirs, [SHARE, SHARE + BLK_DEV])
    shard = jnp.concatenate(
        [mine, their_cache, mine_powers, their_powers, *by_core(mine_q, their_q)], axis=0
    ).astype(jnp.float16)
    gathered = lax.all_gather(shard, SEQ, axis_index_groups=KV_LINES, tiled=True)
    parts = gathered.reshape(LINE, SHARD, HEAD)
    lists = lax.ppermute(parts[:, SHARD - 2 * QROWS :], "core", swap)
    lists = lists.reshape(2 * LINE * QROWS, HEAD).astype(jnp.bfloat16)
    cache = gathered.astype(jnp.bfloat16)
    powers = parts[:, CACHE : CACHE + 2 * BLK_DEV].reshape(2 * LINE * BLK_DEV, HEAD).astype(jnp.float32)

    coded = lists.reshape(2 * LINE, QROWS, HEAD)[:, ROWS + 4, : 2 * TOPK].astype(jnp.int32)
    wanted = coded[:, :TOPK] * 64 + coded[:, TOPK:]
    owner, local = wanted // BLK_DEV, wanted % BLK_DEV
    owner_z, owner_y, owner_core = owner // (2 * Y), (owner // 2) % Y, owner % 2
    my_z, my_y, my_core = (placed[i : i + 1, :TOPK] for i in range(3))
    here = jnp.where(my_core == 0, owner_z == my_z, owner_y == my_y)
    position = jnp.where(my_core == 0, owner_y, owner_z)
    index = (position * 2 + (owner_core != my_core).astype(jnp.int32)) * BLK_DEV + local
    rank = jnp.sum(
        (here[:, None, :] & (jnp.arange(TOPK)[None, None, :] < jnp.arange(TOPK)[None, :, None])).astype(jnp.int32),
        axis=2,
    )
    match = here[:, :, None] & (rank[:, :, None] == jnp.arange(BLK_DEV)[None, None, :])
    indices = jnp.sum(jnp.where(match, index[:, :, None], 0), axis=1)
    places = (indices // (2 * BLK_DEV)) * SHARD + (indices % (2 * BLK_DEV)) * PAIR
    counts = jnp.sum(here.astype(jnp.int32), axis=1)

    partial = pl.pallas_call(
        memory_kernel,
        out_shape=pltpu.HBM((LINE, OROWS, ROWS), jnp.bfloat16),
        in_specs=[smem] * 3 + [vmem] * 3 + [pl.BlockSpec(memory_space=pl.ANY)],
        out_specs=pl.BlockSpec(memory_space=pltpu.HBM),
        scratch_shapes=[
            pltpu.VMEM((2, OROWS, ROWS), jnp.bfloat16),
            pltpu.VMEM((2, ROWS, HEAD), jnp.bfloat16),
            pltpu.VMEM((2, HEAD, ROWS), jnp.float32),
            pltpu.VMEM((2, 1, ROWS), jnp.float32),
            pltpu.VMEM((2, 1, ROWS), jnp.float32),
            pltpu.SemaphoreType.DMA((2,)),
        ],
        compiler_params=pltpu.CompilerParams(vmem_limit_bytes=24 << 20),
        cost_estimate=pl.CostEstimate(
            flops=4 * 64 * ROWS * BLOCK * HEAD, bytes_accessed=6 << 20, transcendentals=64 * ROWS * BLOCK
        ),
        name="memory",
    )(counts, places, indices, lists, powers, cache, near)
    returned = lax.all_to_all(
        partial, SEQ, split_axis=0, concat_axis=0, axis_index_groups=Q_LINES, tiled=True
    )

    window = pl.pallas_call(
        window_kernel,
        out_shape=jax.ShapeDtypeStruct((2, HEAD, ROWS), jnp.float32),
        in_specs=[smem] + [vmem] * 3,
        out_specs=vmem,
        compiler_params=pltpu.CompilerParams(vmem_limit_bytes=16 << 20),
        cost_estimate=pl.CostEstimate(
            flops=4 * 2 * ROWS * 256 * HEAD, bytes_accessed=1 << 20, transcendentals=2 * ROWS * 256
        ),
        name="window",
    )(
        where,
        by_head,
        jnp.concatenate([near[:, :128], keys.transpose(1, 0, 2)], axis=1),
        jnp.concatenate([near[:, 128:], values.transpose(1, 0, 2)], axis=1),
    )
    their_window = lax.ppermute(window[1], "core", swap)

    gate = jax.nn.sigmoid(gate_logits).reshape(2, 4)
    gate = jnp.repeat(jnp.where(first_core, gate[0], gate[1]), 128)[None, :]
    mixed = pl.pallas_call(
        merge_kernel,
        out_shape=jax.ShapeDtypeStruct((2 * X, 32, ROWS), jnp.bfloat16),
        in_specs=[smem] + [vmem] * 4,
        out_specs=vmem,
        compiler_params=pltpu.CompilerParams(vmem_limit_bytes=16 << 20),
        cost_estimate=pl.CostEstimate(flops=1 << 22, bytes_accessed=4 << 20, transcendentals=1 << 13),
        name="merge",
    )(where, returned, window, their_window, gate)
    rows = lax.all_to_all(mixed, ("head", "core"), split_axis=0, concat_axis=0, tiled=True)
    return rows.transpose(1, 0, 2).reshape(32, 2 * X * ROWS)


def solution(mesh):
    fine = Mesh(mesh.devices.reshape(Z, Y, 2, X), ("z", "y", "core", "head"))
    placed = (
        P(SEQ, "head", None),
        P(SEQ, "head", None),
        P(SEQ, "head", None),
        P(SEQ, "head", None),
        P(SEQ, "head", None),
        P("head", SEQ, None),
        P("head"),
    )
    return jax.shard_map(
        on_device, mesh=fine, in_specs=placed, out_specs=P(SEQ + ("head",), None), check_vma=False
    )
```

```python
import functools
import math

import jax
import jax.numpy as jnp
from jax import lax
from jax.experimental import pallas as pl
from jax.experimental.pallas import tpu as pltpu
from jax.sharding import Mesh
from jax.sharding import PartitionSpec as P

Z, Y, X = 8, 8, 4
LINE = 8
BLOCK = 64
TOPK = 32
BLK_DEV = 16
HEAD = 128
ROWS = 512
QROWS = ROWS + 16
PAIR = 2 * BLOCK
SHARE = BLK_DEV * PAIR
CACHE = 2 * SHARE
SHARD = CACHE + 2 * BLK_DEV + 2 * QROWS
OROWS = 2 * HEAD + 16
STEP = 8
LOWEST = -3.0e38
EXPO = HEAD**-0.5 * math.log2(math.e)
SEQ = ("z", "y", "core")


def seq_index(z, y, core):
    return (z * Y + y) * 2 + core


Y_LINES = [[[seq_index(z, y, core) for y in range(Y)] for z in range(Z)] for core in range(2)]
Z_LINES = [[[seq_index(z, y, core) for z in range(Z)] for y in range(Y)] for core in range(2)]
KV_LINES = Y_LINES[0] + Z_LINES[1]
Q_LINES = Z_LINES[0] + Y_LINES[1]


def scaled(x):
    largest = jnp.max(jnp.abs(x), axis=1, keepdims=True)
    power = 14.0 - jnp.floor(jnp.log2(jnp.maximum(largest, 1e-37)))
    power = jnp.clip(power, -113.0, 126.0)
    return (x * jnp.exp2(power)).astype(jnp.bfloat16), power


def pack_cache(k_ref, v_ref, head, out_ref):
    lane = lax.broadcasted_iota(jnp.int32, (128, 128), 1)
    powers = jnp.zeros((128, 128), jnp.float32)
    for b in range(BLK_DEV):
        at = slice(b * BLOCK, (b + 1) * BLOCK)
        rows = jnp.concatenate([k_ref[head, at, :], v_ref[head, at, :]], axis=0).astype(jnp.float32)
        out_ref[b * PAIR : (b + 1) * PAIR, :], power = scaled(rows)
        powers = jnp.where(lane == b, power, powers)
    return powers.T[:BLK_DEV, :].astype(jnp.bfloat16)


def pack_queries(q_ref, ids_ref, head, out_ref, first):
    lane = lax.broadcasted_iota(jnp.int32, (128, 128), 1)
    powers = jnp.zeros((128, 128), jnp.float32)
    for i in range(ROWS // 128):
        rows = q_ref[head, i * 128 : (i + 1) * 128, :].astype(jnp.float32)
        out_ref[first + i * 128 : first + (i + 1) * 128, :], power = scaled(rows)
        powers = jnp.where(lane == i, power, powers)
    ids = ids_ref[head]
    coded = jnp.concatenate([ids >> 6, ids & 63, jnp.zeros((1, HEAD - 2 * TOPK), jnp.int32)], axis=1)
    row = lax.broadcasted_iota(jnp.int32, (16, 128), 0)
    extra = jnp.where(row == ROWS // 128, coded.astype(jnp.float32), powers.T[:16, :])
    out_ref[first + ROWS : first + QROWS, :] = extra.astype(jnp.bfloat16)


def pack_other_kernel(where_ref, k_ref, v_ref, q_ref, ids_ref, other_ref, place_ref):
    for i in range(3):
        place_ref[i : i + 1, :] = jnp.full((1, 128), where_ref[i], jnp.int32)
    core = where_ref[2]
    other_ref[SHARE : SHARE + BLK_DEV, :] = pack_cache(k_ref, v_ref, 1 - core, other_ref)
    pack_queries(q_ref, ids_ref, core, other_ref, SHARE + BLK_DEV)


def pack_mine_kernel(where_ref, k_ref, v_ref, q_ref, ids_ref, mine_ref, powers_ref, queries_ref):
    core = where_ref[2]
    powers_ref[...] = pack_cache(k_ref, v_ref, core, mine_ref)
    pack_queries(q_ref, ids_ref, 1 - core, queries_ref, 0)


def window_kernel(where_ref, q_ref, k_ref, v_ref, o_ref):
    has_before = where_ref[0] + where_ref[1] + where_ref[2] > 0
    for head in range(2):
        s = lax.dot_general(
            k_ref[head], q_ref[head], (((1,), (1,)), ((), ())), preferred_element_type=jnp.float32
        )
        kpos = lax.broadcasted_iota(jnp.int32, s.shape, 0) - 128
        qpos = lax.broadcasted_iota(jnp.int32, s.shape, 1) & 127
        allowed = (kpos <= qpos) & (kpos > qpos - 128) & ((kpos >= 0) | has_before)
        s = jnp.where(allowed, s, LOWEST)
        top = jnp.max(s, axis=0, keepdims=True)
        p = jnp.exp2((s - top) * EXPO)
        total = jnp.sum(p, axis=0, keepdims=True)
        out = lax.dot_general(
            v_ref[head], p.astype(jnp.bfloat16), (((0,), (0,)), ((), ())), preferred_element_type=jnp.float32
        )
        o_ref[head ^ where_ref[2]] = out / total


def memory_kernel(count_ref, place_ref, power_at_ref, q_ref, powers_ref, kv_ref, near_ref, o_ref, stage, q_buf, acc, top_s, sum_s, out_sems):
    eye = lax.broadcasted_iota(jnp.int32, (128, 128), 0) == lax.broadcasted_iota(jnp.int32, (128, 128), 1)
    low = lax.broadcasted_iota(jnp.int32, (1, 128), 1) < BLOCK

    def back(x, power_row):
        scale = jnp.where(eye, jnp.exp2(-power_row), 0.0).astype(jnp.bfloat16)
        return jnp.dot(scale, x, preferred_element_type=jnp.float32).astype(jnp.bfloat16)

    def send(peer):
        return pltpu.make_async_copy(stage.at[peer % 2], o_ref.at[peer], out_sems.at[peer % 2])

    def attend(index, rc, count, step):
        keys, values = [], []
        for i in range(0, STEP, 2):
            places = [pl.multiple_of(place_ref[index, step * STEP + i + j], 16) for j in range(2)]
            rows = [powers_ref[pl.ds(power_at_ref[index, step * STEP + i + j], 1), :] for j in range(2)]
            turned = [pltpu.roll(row, BLOCK, 1) for row in rows]
            both = jnp.concatenate([kv_ref[pl.ds(at, BLOCK), :] for at in places], axis=0)
            keys.append(back(both, jnp.where(low, rows[0], turned[1])))
            both = jnp.concatenate([kv_ref[pl.ds(at + BLOCK, BLOCK), :] for at in places], axis=0)
            down = jnp.exp2(-jnp.where(low, turned[0], rows[1]))
            values.append((both.T.astype(jnp.float32) * down).astype(jnp.bfloat16))
        s = lax.dot_general(
            jnp.concatenate(keys, axis=0), q_buf[rc], (((1,), (1,)), ((), ())), preferred_element_type=jnp.float32
        )
        s = jnp.concatenate(
            [
                jnp.where(step * STEP + i < count, s[i * BLOCK : (i + 1) * BLOCK], LOWEST)
                for i in range(STEP)
            ],
            axis=0,
        )
        top = jnp.max(s, axis=0, keepdims=True)
        return s, top, jnp.concatenate(values, axis=1)

    for peer in range(LINE):
        slot = peer % 2
        counts = [count_ref[peer * 2 + rc] for rc in range(2)]
        for rc in range(2):
            index = peer * 2 + rc
            first = index * QROWS
            extra = q_ref[first + ROWS : first + QROWS, :].astype(jnp.float32)
            for i in range(ROWS // 128):
                q_buf[rc, i * 128 : (i + 1) * 128, :] = back(
                    q_ref[first + i * 128 : first + (i + 1) * 128, :], extra[i : i + 1, :]
                )
        held = [attend(peer * 2 + rc, rc, counts[rc], 0) for rc in range(2)]
        for rc in range(2):
            s, top, values = held[rc]
            p = jnp.exp2((s - top) * EXPO)
            top_s[rc] = top
            sum_s[rc] = jnp.sum(p, axis=0, keepdims=True)
            acc[rc] = jnp.dot(values, p.astype(jnp.bfloat16), preferred_element_type=jnp.float32)

        def one_step(step, carry):
            for rc in range(2):
                s, top, values = attend(peer * 2 + rc, rc, counts[rc], step)
                top = jnp.maximum(top_s[rc], top)
                p = jnp.exp2((s - top) * EXPO)
                alpha = jnp.exp2((top_s[rc] - top) * EXPO)
                top_s[rc] = top
                sum_s[rc] = sum_s[rc] * alpha + jnp.sum(p, axis=0, keepdims=True)
                acc[rc] = acc[rc] * alpha + jnp.dot(values, p.astype(jnp.bfloat16), preferred_element_type=jnp.float32)
            return carry

        lax.fori_loop(1, (jnp.maximum(counts[0], counts[1]) + STEP - 1) // STEP, one_step, 0)
        if peer >= 2:
            send(peer - 2).wait()
        rows = lax.broadcasted_iota(jnp.int32, (16, ROWS), 0)
        pieces = jnp.zeros((16, ROWS), jnp.float32)
        for rc in range(2):
            some = counts[rc] > 0
            total = jnp.where(some, sum_s[rc], 1.0)
            stage[slot, rc * HEAD : (rc + 1) * HEAD, :] = (acc[rc] * jnp.where(some, 1.0 / total, 0.0)).astype(jnp.bfloat16)
            level = jnp.where(some, top_s[rc] * EXPO + jnp.log2(total), LOWEST)
            high = level.astype(jnp.bfloat16).astype(jnp.float32)
            mid = (level - high).astype(jnp.bfloat16).astype(jnp.float32)
            for i, piece in enumerate((high, mid, level - high - mid)):
                pieces = jnp.where(rows == 3 * rc + i, piece, pieces)
        stage[slot, 2 * HEAD :, :] = pieces.astype(jnp.bfloat16)
        send(peer).start()
    send(LINE - 2).wait()
    send(LINE - 1).wait()


def merge_kernel(where_ref, part_ref, window_ref, their_window_ref, gate_ref, o_ref):
    gate = gate_ref[...]
    for i, near in enumerate((window_ref.at[0], their_window_ref)):
        rc = where_ref[2] ^ i
        at = pl.ds(pl.multiple_of(rc * HEAD, HEAD), HEAD)
        levels = []
        for peer in range(LINE):
            pieces = part_ref[peer, 2 * HEAD :, :].astype(jnp.float32)
            pieces = jnp.where(rc == 0, pieces[0:3, :], pieces[3:6, :])
            levels.append(pieces[0:1] + pieces[1:2] + pieces[2:3])
        top = functools.reduce(jnp.maximum, levels)
        shares = [jnp.exp2(level - top) for level in levels]
        scale = gate / functools.reduce(jnp.add, shares)
        mixed = (1.0 - gate) * near[...]
        for peer in range(LINE):
            mixed = mixed + part_ref[peer, at, :].astype(jnp.float32) * (shares[peer] * scale)
        for g in range(4):
            flat = mixed[:, g * 128 : (g + 1) * 128].T.astype(jnp.bfloat16)
            for x in range(X):
                o_ref[x * 2 + rc, :, g * 128 : (g + 1) * 128] = flat[x * 32 : (x + 1) * 32, :]


def on_device(queries, keys, values, mem_keys, mem_values, mem_ids, gate_logits):
    z, y, core = lax.axis_index("z"), lax.axis_index("y"), lax.axis_index("core")
    first_core = core == 0
    smem = pl.BlockSpec(memory_space=pltpu.SMEM)
    vmem = pl.BlockSpec(memory_space=pltpu.VMEM)
    swap = [(0, 1), (1, 0)]

    def by_core(mine, other):
        return jnp.where(first_core, mine, other), jnp.where(first_core, other, mine)

    where = jnp.stack([z, y, core]).astype(jnp.int32)
    by_head = queries.reshape(128, 2, 4, HEAD).transpose(1, 2, 0, 3).reshape(2, ROWS, HEAD)
    packed = (where, mem_keys.transpose(1, 0, 2), mem_values.transpose(1, 0, 2), by_head, mem_ids)

    def pack(kernel, name, *shapes):
        return pl.pallas_call(
            kernel,
            out_shape=[jax.ShapeDtypeStruct(*shape) for shape in shapes],
            in_specs=[smem] + [vmem] * 4,
            out_specs=[vmem] * len(shapes),
            compiler_params=pltpu.CompilerParams(vmem_limit_bytes=16 << 20),
            cost_estimate=pl.CostEstimate(flops=1 << 22, bytes_accessed=2 << 20, transcendentals=1 << 13),
            name=name,
        )(*packed)

    other, placed = pack(
        pack_other_kernel,
        "pack_other",
        ((SHARE + BLK_DEV + QROWS, HEAD), jnp.bfloat16),
        ((8, 128), jnp.int32),
    )
    mine, mine_powers, mine_q = pack(
        pack_mine_kernel,
        "pack_mine",
        ((SHARE, HEAD), jnp.bfloat16),
        ((BLK_DEV, HEAD), jnp.bfloat16),
        ((QROWS, HEAD), jnp.bfloat16),
    )
    near = lax.ppermute(
        jnp.concatenate([keys, values], axis=0).transpose(1, 0, 2), SEQ, [(i, i + 1) for i in range(2 * Z * Y - 1)]
    )
    theirs = lax.ppermute(other, "core", swap)
    their_cache, their_powers, their_q = jnp.split(theirs, [SHARE, SHARE + BLK_DEV])
    shard = jnp.concatenate(
        [mine, their_cache, mine_powers, their_powers, *by_core(mine_q, their_q)], axis=0
    ).astype(jnp.float16)
    gathered = lax.all_gather(shard, SEQ, axis_index_groups=KV_LINES, tiled=True)
    parts = gathered.reshape(LINE, SHARD, HEAD)
    lists = lax.ppermute(parts[:, SHARD - 2 * QROWS :], "core", swap)
    lists = lists.reshape(2 * LINE * QROWS, HEAD).astype(jnp.bfloat16)
    cache = gathered.astype(jnp.bfloat16)
    powers = parts[:, CACHE : CACHE + 2 * BLK_DEV].reshape(2 * LINE * BLK_DEV, HEAD).astype(jnp.float32)

    coded = lists.reshape(2 * LINE, QROWS, HEAD)[:, ROWS + 4, : 2 * TOPK].astype(jnp.int32)
    wanted = coded[:, :TOPK] * 64 + coded[:, TOPK:]
    owner, local = wanted // BLK_DEV, wanted % BLK_DEV
    owner_z, owner_y, owner_core = owner // (2 * Y), (owner // 2) % Y, owner % 2
    my_z, my_y, my_core = (placed[i : i + 1, :TOPK] for i in range(3))
    here = jnp.where(my_core == 0, owner_z == my_z, owner_y == my_y)
    position = jnp.where(my_core == 0, owner_y, owner_z)
    index = (position * 2 + (owner_core != my_core).astype(jnp.int32)) * BLK_DEV + local
    rank = jnp.sum(
        (here[:, None, :] & (jnp.arange(TOPK)[None, None, :] < jnp.arange(TOPK)[None, :, None])).astype(jnp.int32),
        axis=2,
    )
    match = here[:, :, None] & (rank[:, :, None] == jnp.arange(BLK_DEV)[None, None, :])
    indices = jnp.sum(jnp.where(match, index[:, :, None], 0), axis=1)
    places = (indices // (2 * BLK_DEV)) * SHARD + (indices % (2 * BLK_DEV)) * PAIR
    counts = jnp.sum(here.astype(jnp.int32), axis=1)

    partial = pl.pallas_call(
        memory_kernel,
        out_shape=pltpu.HBM((LINE, OROWS, ROWS), jnp.bfloat16),
        in_specs=[smem] * 3 + [vmem] * 3 + [pl.BlockSpec(memory_space=pl.ANY)],
        out_specs=pl.BlockSpec(memory_space=pltpu.HBM),
        scratch_shapes=[
            pltpu.VMEM((2, OROWS, ROWS), jnp.bfloat16),
            pltpu.VMEM((2, ROWS, HEAD), jnp.bfloat16),
            pltpu.VMEM((2, HEAD, ROWS), jnp.float32),
            pltpu.VMEM((2, 1, ROWS), jnp.float32),
            pltpu.VMEM((2, 1, ROWS), jnp.float32),
            pltpu.SemaphoreType.DMA((2,)),
        ],
        compiler_params=pltpu.CompilerParams(vmem_limit_bytes=24 << 20),
        cost_estimate=pl.CostEstimate(
            flops=4 * 64 * ROWS * BLOCK * HEAD, bytes_accessed=6 << 20, transcendentals=64 * ROWS * BLOCK
        ),
        name="memory",
    )(counts, places, indices, lists, powers, cache, near)
    returned = lax.all_to_all(
        partial, SEQ, split_axis=0, concat_axis=0, axis_index_groups=Q_LINES, tiled=True
    )

    window = pl.pallas_call(
        window_kernel,
        out_shape=jax.ShapeDtypeStruct((2, HEAD, ROWS), jnp.float32),
        in_specs=[smem] + [vmem] * 3,
        out_specs=vmem,
        compiler_params=pltpu.CompilerParams(vmem_limit_bytes=16 << 20),
        cost_estimate=pl.CostEstimate(
            flops=4 * 2 * ROWS * 256 * HEAD, bytes_accessed=1 << 20, transcendentals=2 * ROWS * 256
        ),
        name="window",
    )(
        where,
        by_head,
        jnp.concatenate([near[:, :128], keys.transpose(1, 0, 2)], axis=1),
        jnp.concatenate([near[:, 128:], values.transpose(1, 0, 2)], axis=1),
    )
    their_window = lax.ppermute(window[1], "core", swap)

    gate = jax.nn.sigmoid(gate_logits).reshape(2, 4)
    gate = jnp.repeat(jnp.where(first_core, gate[0], gate[1]), 128)[None, :]
    mixed = pl.pallas_call(
        merge_kernel,
        out_shape=jax.ShapeDtypeStruct((2 * X, 32, ROWS), jnp.bfloat16),
        in_specs=[smem] + [vmem] * 4,
        out_specs=vmem,
        compiler_params=pltpu.CompilerParams(vmem_limit_bytes=16 << 20),
        cost_estimate=pl.CostEstimate(flops=1 << 22, bytes_accessed=4 << 20, transcendentals=1 << 13),
        name="merge",
    )(where, returned, window, their_window, gate)
    rows = lax.all_to_all(mixed, ("head", "core"), split_axis=0, concat_axis=0, tiled=True)
    return rows.transpose(1, 0, 2).reshape(32, 2 * X * ROWS)


def solution(mesh):
    fine = Mesh(mesh.devices.reshape(Z, Y, 2, X), ("z", "y", "core", "head"))
    placed = (
        P(SEQ, "head", None),
        P(SEQ, "head", None),
        P(SEQ, "head", None),
        P(SEQ, "head", None),
        P(SEQ, "head", None),
        P("head", SEQ, None),
        P("head"),
    )
    return jax.shard_map(
        on_device, mesh=fine, in_specs=placed, out_specs=P(SEQ + ("head",), None), check_vma=False
    )
```

```python
import functools
import math

import jax
import jax.numpy as jnp
from jax import lax
from jax.experimental import pallas as pl
from jax.experimental.pallas import tpu as pltpu
from jax.sharding import Mesh
from jax.sharding import PartitionSpec as P

Z, Y, X = 8, 8, 4
LINE = 8
BLOCK = 64
TOPK = 32
BLK_DEV = 16
HEAD = 128
ROWS = 512
QROWS = ROWS + 16
PAIR = 2 * BLOCK
SHARE = BLK_DEV * PAIR
CACHE = 2 * SHARE
SHARD = CACHE + 2 * BLK_DEV + 2 * QROWS
OROWS = 2 * HEAD + 16
STEP = 8
LOWEST = -3.0e38
EXPO = HEAD**-0.5 * math.log2(math.e)
SEQ = ("z", "y", "core")


def seq_index(z, y, core):
    return (z * Y + y) * 2 + core


Y_LINES = [[[seq_index(z, y, core) for y in range(Y)] for z in range(Z)] for core in range(2)]
Z_LINES = [[[seq_index(z, y, core) for z in range(Z)] for y in range(Y)] for core in range(2)]
KV_LINES = Y_LINES[0] + Z_LINES[1]
Q_LINES = Z_LINES[0] + Y_LINES[1]


def scaled(x):
    largest = jnp.max(jnp.abs(x), axis=1, keepdims=True)
    power = 14.0 - jnp.floor(jnp.log2(jnp.maximum(largest, 1e-37)))
    power = jnp.clip(power, -113.0, 126.0)
    return (x * jnp.exp2(power)).astype(jnp.bfloat16), power


def pack_cache(k_ref, v_ref, head, out_ref):
    lane = lax.broadcasted_iota(jnp.int32, (128, 128), 1)
    powers = jnp.zeros((128, 128), jnp.float32)
    for b in range(BLK_DEV):
        at = slice(b * BLOCK, (b + 1) * BLOCK)
        rows = jnp.concatenate([k_ref[head, at, :], v_ref[head, at, :]], axis=0).astype(jnp.float32)
        out_ref[b * PAIR : (b + 1) * PAIR, :], power = scaled(rows)
        powers = jnp.where(lane == b, power, powers)
    return powers.T[:BLK_DEV, :].astype(jnp.bfloat16)


def pack_queries(q_ref, ids_ref, head, out_ref, first):
    lane = lax.broadcasted_iota(jnp.int32, (128, 128), 1)
    powers = jnp.zeros((128, 128), jnp.float32)
    for i in range(ROWS // 128):
        rows = q_ref[head, i * 128 : (i + 1) * 128, :].astype(jnp.float32)
        out_ref[first + i * 128 : first + (i + 1) * 128, :], power = scaled(rows)
        powers = jnp.where(lane == i, power, powers)
    ids = ids_ref[head]
    coded = jnp.concatenate([ids >> 6, ids & 63, jnp.zeros((1, HEAD - 2 * TOPK), jnp.int32)], axis=1)
    row = lax.broadcasted_iota(jnp.int32, (16, 128), 0)
    extra = jnp.where(row == ROWS // 128, coded.astype(jnp.float32), powers.T[:16, :])
    out_ref[first + ROWS : first + QROWS, :] = extra.astype(jnp.bfloat16)


def pack_other_kernel(where_ref, k_ref, v_ref, q_ref, ids_ref, other_ref, place_ref):
    for i in range(3):
        place_ref[i : i + 1, :] = jnp.full((1, 128), where_ref[i], jnp.int32)
    core = where_ref[2]
    other_ref[SHARE : SHARE + BLK_DEV, :] = pack_cache(k_ref, v_ref, 1 - core, other_ref)
    pack_queries(q_ref, ids_ref, core, other_ref, SHARE + BLK_DEV)


def pack_mine_kernel(where_ref, k_ref, v_ref, q_ref, ids_ref, mine_ref, powers_ref, queries_ref):
    core = where_ref[2]
    powers_ref[...] = pack_cache(k_ref, v_ref, core, mine_ref)
    pack_queries(q_ref, ids_ref, 1 - core, queries_ref, 0)


def window_kernel(where_ref, q_ref, k_ref, v_ref, o_ref):
    has_before = where_ref[0] + where_ref[1] + where_ref[2] > 0
    for head in range(2):
        s = lax.dot_general(
            k_ref[head], q_ref[head], (((1,), (1,)), ((), ())), preferred_element_type=jnp.float32
        )
        kpos = lax.broadcasted_iota(jnp.int32, s.shape, 0) - 128
        qpos = lax.broadcasted_iota(jnp.int32, s.shape, 1) & 127
        allowed = (kpos <= qpos) & (kpos > qpos - 128) & ((kpos >= 0) | has_before)
        s = jnp.where(allowed, s, LOWEST)
        top = jnp.max(s, axis=0, keepdims=True)
        p = jnp.exp2((s - top) * EXPO)
        total = jnp.sum(p, axis=0, keepdims=True)
        out = lax.dot_general(
            v_ref[head], p.astype(jnp.bfloat16), (((0,), (0,)), ((), ())), preferred_element_type=jnp.float32
        )
        o_ref[head ^ where_ref[2]] = out / total


def memory_kernel(count_ref, place_ref, power_at_ref, q_ref, powers_ref, kv_ref, near_ref, o_ref, stage, q_buf, acc, top_s, sum_s, out_sems):
    eye = lax.broadcasted_iota(jnp.int32, (128, 128), 0) == lax.broadcasted_iota(jnp.int32, (128, 128), 1)
    low = lax.broadcasted_iota(jnp.int32, (1, 128), 1) < BLOCK

    def back(x, power_row):
        scale = jnp.where(eye, jnp.exp2(-power_row), 0.0).astype(jnp.bfloat16)
        return jnp.dot(scale, x, preferred_element_type=jnp.float32).astype(jnp.bfloat16)

    def send(peer):
        return pltpu.make_async_copy(stage.at[peer % 2], o_ref.at[peer], out_sems.at[peer % 2])

    def attend(index, rc, count, step):
        keys, values = [], []
        for i in range(0, STEP, 2):
            places = [pl.multiple_of(place_ref[index, step * STEP + i + j], 16) for j in range(2)]
            rows = [powers_ref[pl.ds(power_at_ref[index, step * STEP + i + j], 1), :] for j in range(2)]
            turned = [pltpu.roll(row, BLOCK, 1) for row in rows]
            both = jnp.concatenate([kv_ref[pl.ds(at, BLOCK), :] for at in places], axis=0)
            keys.append(back(both, jnp.where(low, rows[0], turned[1])))
            both = jnp.concatenate([kv_ref[pl.ds(at + BLOCK, BLOCK), :] for at in places], axis=0)
            down = jnp.exp2(-jnp.where(low, turned[0], rows[1]))
            values.append((both.T.astype(jnp.float32) * down).astype(jnp.bfloat16))
        s = lax.dot_general(
            jnp.concatenate(keys, axis=0), q_buf[rc], (((1,), (1,)), ((), ())), preferred_element_type=jnp.float32
        )
        s = jnp.concatenate(
            [
                jnp.where(step * STEP + i < count, s[i * BLOCK : (i + 1) * BLOCK], LOWEST)
                for i in range(STEP)
            ],
            axis=0,
        )
        top = jnp.max(s, axis=0, keepdims=True)
        return s, top, jnp.concatenate(values, axis=1)

    for peer in range(LINE):
        slot = peer % 2
        counts = [count_ref[peer * 2 + rc] for rc in range(2)]
        for rc in range(2):
            index = peer * 2 + rc
            first = index * QROWS
            extra = q_ref[first + ROWS : first + QROWS, :].astype(jnp.float32)
            for i in range(ROWS // 128):
                q_buf[rc, i * 128 : (i + 1) * 128, :] = back(
                    q_ref[first + i * 128 : first + (i + 1) * 128, :], extra[i : i + 1, :]
                )
        held = [attend(peer * 2 + rc, rc, counts[rc], 0) for rc in range(2)]
        for rc in range(2):
            s, top, values = held[rc]
            p = jnp.exp2((s - top) * EXPO)
            top_s[rc] = top
            sum_s[rc] = jnp.sum(p, axis=0, keepdims=True)
            acc[rc] = jnp.dot(values, p.astype(jnp.bfloat16), preferred_element_type=jnp.float32)

        def one_step(step, carry):
            for rc in range(2):
                s, top, values = attend(peer * 2 + rc, rc, counts[rc], step)
                top = jnp.maximum(top_s[rc], top)
                p = jnp.exp2((s - top) * EXPO)
                alpha = jnp.exp2((top_s[rc] - top) * EXPO)
                top_s[rc] = top
                sum_s[rc] = sum_s[rc] * alpha + jnp.sum(p, axis=0, keepdims=True)
                acc[rc] = acc[rc] * alpha + jnp.dot(values, p.astype(jnp.bfloat16), preferred_element_type=jnp.float32)
            return carry

        lax.fori_loop(1, (jnp.maximum(counts[0], counts[1]) + STEP - 1) // STEP, one_step, 0)
        if peer >= 2:
            send(peer - 2).wait()
        rows = lax.broadcasted_iota(jnp.int32, (16, ROWS), 0)
        pieces = jnp.zeros((16, ROWS), jnp.float32)
        for rc in range(2):
            some = counts[rc] > 0
            total = jnp.where(some, sum_s[rc], 1.0)
            stage[slot, rc * HEAD : (rc + 1) * HEAD, :] = (acc[rc] * jnp.where(some, 1.0 / total, 0.0)).astype(jnp.bfloat16)
            level = jnp.where(some, top_s[rc] * EXPO + jnp.log2(total), LOWEST)
            high = level.astype(jnp.bfloat16).astype(jnp.float32)
            mid = (level - high).astype(jnp.bfloat16).astype(jnp.float32)
            for i, piece in enumerate((high, mid, level - high - mid)):
                pieces = jnp.where(rows == 3 * rc + i, piece, pieces)
        stage[slot, 2 * HEAD :, :] = pieces.astype(jnp.bfloat16)
        send(peer).start()
    send(LINE - 2).wait()
    send(LINE - 1).wait()


def merge_kernel(place_ref, part_ref, window_ref, their_window_ref, gate_ref, o_ref):
    gate = gate_ref[...]
    first_core = place_ref[2:3, 0:1] == 0
    for rc in range(2):
        at = slice(rc * HEAD, (rc + 1) * HEAD)
        near = jnp.where(first_core == (rc == 0), window_ref[0], their_window_ref[...])
        levels = []
        for peer in range(LINE):
            pieces = part_ref[peer, 2 * HEAD :, :].astype(jnp.float32)
            pieces = pieces[3 * rc : 3 * rc + 3, :]
            levels.append(pieces[0:1] + pieces[1:2] + pieces[2:3])
        top = functools.reduce(jnp.maximum, levels)
        shares = [jnp.exp2(level - top) for level in levels]
        scale = gate / functools.reduce(jnp.add, shares)
        mixed = (1.0 - gate) * near
        for peer in range(LINE):
            mixed = mixed + part_ref[peer, at, :].astype(jnp.float32) * (shares[peer] * scale)
        for g in range(4):
            flat = mixed[:, g * 128 : (g + 1) * 128].T.astype(jnp.bfloat16)
            for x in range(X):
                o_ref[x * 2 + rc, :, g * 128 : (g + 1) * 128] = flat[x * 32 : (x + 1) * 32, :]


def on_device(queries, keys, values, mem_keys, mem_values, mem_ids, gate_logits):
    z, y, core = lax.axis_index("z"), lax.axis_index("y"), lax.axis_index("core")
    first_core = core == 0
    smem = pl.BlockSpec(memory_space=pltpu.SMEM)
    vmem = pl.BlockSpec(memory_space=pltpu.VMEM)
    swap = [(0, 1), (1, 0)]

    def by_core(mine, other):
        return jnp.where(first_core, mine, other), jnp.where(first_core, other, mine)

    where = jnp.stack([z, y, core]).astype(jnp.int32)
    by_head = queries.reshape(128, 2, 4, HEAD).transpose(1, 2, 0, 3).reshape(2, ROWS, HEAD)
    packed = (where, mem_keys.transpose(1, 0, 2), mem_values.transpose(1, 0, 2), by_head, mem_ids)

    def pack(kernel, name, *shapes):
        return pl.pallas_call(
            kernel,
            out_shape=[jax.ShapeDtypeStruct(*shape) for shape in shapes],
            in_specs=[smem] + [vmem] * 4,
            out_specs=[vmem] * len(shapes),
            compiler_params=pltpu.CompilerParams(vmem_limit_bytes=16 << 20),
            cost_estimate=pl.CostEstimate(flops=1 << 22, bytes_accessed=2 << 20, transcendentals=1 << 13),
            name=name,
        )(*packed)

    other, placed = pack(
        pack_other_kernel,
        "pack_other",
        ((SHARE + BLK_DEV + QROWS, HEAD), jnp.bfloat16),
        ((8, 128), jnp.int32),
    )
    mine, mine_powers, mine_q = pack(
        pack_mine_kernel,
        "pack_mine",
        ((SHARE, HEAD), jnp.bfloat16),
        ((BLK_DEV, HEAD), jnp.bfloat16),
        ((QROWS, HEAD), jnp.bfloat16),
    )
    near = lax.ppermute(
        jnp.concatenate([keys, values], axis=0).transpose(1, 0, 2), SEQ, [(i, i + 1) for i in range(2 * Z * Y - 1)]
    )
    theirs = lax.ppermute(other, "core", swap)
    their_cache, their_powers, their_q = jnp.split(theirs, [SHARE, SHARE + BLK_DEV])
    shard = jnp.concatenate(
        [mine, their_cache, mine_powers, their_powers, *by_core(mine_q, their_q)], axis=0
    ).astype(jnp.float16)
    gathered = lax.all_gather(shard, SEQ, axis_index_groups=KV_LINES, tiled=True)
    parts = gathered.reshape(LINE, SHARD, HEAD)
    lists = lax.ppermute(parts[:, SHARD - 2 * QROWS :], "core", swap)
    lists = lists.reshape(2 * LINE * QROWS, HEAD).astype(jnp.bfloat16)
    cache = gathered.astype(jnp.bfloat16)
    powers = parts[:, CACHE : CACHE + 2 * BLK_DEV].reshape(2 * LINE * BLK_DEV, HEAD).astype(jnp.float32)

    coded = lists.reshape(2 * LINE, QROWS, HEAD)[:, ROWS + 4, : 2 * TOPK].astype(jnp.int32)
    wanted = coded[:, :TOPK] * 64 + coded[:, TOPK:]
    owner, local = wanted // BLK_DEV, wanted % BLK_DEV
    owner_z, owner_y, owner_core = owner // (2 * Y), (owner // 2) % Y, owner % 2
    my_z, my_y, my_core = (placed[i : i + 1, :TOPK] for i in range(3))
    here = jnp.where(my_core == 0, owner_z == my_z, owner_y == my_y)
    position = jnp.where(my_core == 0, owner_y, owner_z)
    index = (position * 2 + (owner_core != my_core).astype(jnp.int32)) * BLK_DEV + local
    rank = jnp.sum(
        (here[:, None, :] & (jnp.arange(TOPK)[None, None, :] < jnp.arange(TOPK)[None, :, None])).astype(jnp.int32),
        axis=2,
    )
    match = here[:, :, None] & (rank[:, :, None] == jnp.arange(BLK_DEV)[None, None, :])
    indices = jnp.sum(jnp.where(match, index[:, :, None], 0), axis=1)
    places = (indices // (2 * BLK_DEV)) * SHARD + (indices % (2 * BLK_DEV)) * PAIR
    counts = jnp.sum(here.astype(jnp.int32), axis=1)

    partial = pl.pallas_call(
        memory_kernel,
        out_shape=pltpu.HBM((LINE, OROWS, ROWS), jnp.bfloat16),
        in_specs=[smem] * 3 + [vmem] * 3 + [pl.BlockSpec(memory_space=pl.ANY)],
        out_specs=pl.BlockSpec(memory_space=pltpu.HBM),
        scratch_shapes=[
            pltpu.VMEM((2, OROWS, ROWS), jnp.bfloat16),
            pltpu.VMEM((2, ROWS, HEAD), jnp.bfloat16),
            pltpu.VMEM((2, HEAD, ROWS), jnp.float32),
            pltpu.VMEM((2, 1, ROWS), jnp.float32),
            pltpu.VMEM((2, 1, ROWS), jnp.float32),
            pltpu.SemaphoreType.DMA((2,)),
        ],
        compiler_params=pltpu.CompilerParams(vmem_limit_bytes=24 << 20),
        cost_estimate=pl.CostEstimate(
            flops=4 * 64 * ROWS * BLOCK * HEAD, bytes_accessed=6 << 20, transcendentals=64 * ROWS * BLOCK
        ),
        name="memory",
    )(counts, places, indices, lists, powers, cache, near)
    returned = lax.all_to_all(
        partial, SEQ, split_axis=0, concat_axis=0, axis_index_groups=Q_LINES, tiled=True
    )

    window = pl.pallas_call(
        window_kernel,
        out_shape=jax.ShapeDtypeStruct((2, HEAD, ROWS), jnp.float32),
        in_specs=[smem] + [vmem] * 3,
        out_specs=vmem,
        compiler_params=pltpu.CompilerParams(vmem_limit_bytes=16 << 20),
        cost_estimate=pl.CostEstimate(
            flops=4 * 2 * ROWS * 256 * HEAD, bytes_accessed=1 << 20, transcendentals=2 * ROWS * 256
        ),
        name="window",
    )(
        where,
        by_head,
        jnp.concatenate([near[:, :128], keys.transpose(1, 0, 2)], axis=1),
        jnp.concatenate([near[:, 128:], values.transpose(1, 0, 2)], axis=1),
    )
    their_window = lax.ppermute(window[1], "core", swap)

    gate = jax.nn.sigmoid(gate_logits).reshape(2, 4)
    gate = jnp.repeat(jnp.where(first_core, gate[0], gate[1]), 128)[None, :]
    mixed = pl.pallas_call(
        merge_kernel,
        out_shape=jax.ShapeDtypeStruct((2 * X, 32, ROWS), jnp.bfloat16),
        in_specs=[vmem] * 5,
        out_specs=vmem,
        compiler_params=pltpu.CompilerParams(vmem_limit_bytes=16 << 20),
        cost_estimate=pl.CostEstimate(flops=1 << 22, bytes_accessed=4 << 20, transcendentals=1 << 13),
        name="merge",
    )(placed, returned, window, their_window, gate)
    rows = lax.all_to_all(mixed, ("head", "core"), split_axis=0, concat_axis=0, tiled=True)
    return rows.transpose(1, 0, 2).reshape(32, 2 * X * ROWS)


def solution(mesh):
    fine = Mesh(mesh.devices.reshape(Z, Y, 2, X), ("z", "y", "core", "head"))
    placed = (
        P(SEQ, "head", None),
        P(SEQ, "head", None),
        P(SEQ, "head", None),
        P(SEQ, "head", None),
        P(SEQ, "head", None),
        P("head", SEQ, None),
        P("head"),
    )
    return jax.shard_map(
        on_device, mesh=fine, in_specs=placed, out_specs=P(SEQ + ("head",), None), check_vma=False
    )
```
